32 devices in a mesh: dp: 2 (over core), expert: 4 (over z), shard: 4 (over y, x).
Axes of the slice: x: 2, y: 2, z: 4, core: 2. Of those that a mesh axis runs over, the one named last changes fastest.
Arguments:
- hidden_in: bfloat16 [6144, 2048], P(('dp', 'expert', 'shard')), may hold values from -6 to 6
- grad_out: bfloat16 [6144, 2048], P(('dp', 'expert', 'shard')), may hold values from -6 to 6
- doc_lengths: int32 [8, 4], P(('dp', 'expert')), may hold values from 1 to 576, as said below
- expert_ids: int32 [6144, 8], P(('dp', 'expert', 'shard')), may hold values from 0 to 15, all different within a row; in each aligned block of 192 rows (0 to 191, 192 to 383, ...) at most 120 rows name the same one
- attn_gain: bfloat16 [2048], P('shard'), may hold values from 0.099609375 to 1.8984375
- query_gain: bfloat16 [2048], P('shard'), may hold values from 0.099609375 to 1.8984375
- key_gain: bfloat16 [2048], P('shard'), may hold values from 0.099609375 to 1.8984375
- mlp_gain: bfloat16 [2048], P('shard'), may hold values from 0.099609375 to 1.8984375
- w_query: bfloat16 [2048, 2048], P('shard'), may hold values from -0.125 to 0.125
- w_key: bfloat16 [2048, 2048], P('shard'), may hold values from -0.125 to 0.125
- w_value: bfloat16 [2048, 2048], P('shard'), may hold values from -0.125 to 0.125
- w_output: bfloat16 [2048, 2048], P('shard'), may hold values from -0.75 to 0.75
- w_router: bfloat16 [2048, 16], P('shard'), may hold values from -0.0625 to 0.0625
- w_gate: bfloat16 [16, 2048, 1024], P(('expert', 'shard'), 'dp'), may hold values from -0.125 to 0.125
- w_up: bfloat16 [16, 2048, 1024], P(('expert', 'shard'), 'dp'), may hold values from -0.125 to 0.125
- w_down: bfloat16 [16, 1024, 2048], P(('expert', 'shard'), None, 'dp'), may hold values from -1 to 1
Outputs:
- block_out: bfloat16 [6144, 2048], P(('dp', 'expert', 'shard'))
- grad_in: float32 [6144, 2048], P(('dp', 'expert', 'shard'))
- grad_attn_gain: float32 [2048], P('shard')
- grad_query_gain: float32 [2048], P('shard')
- grad_key_gain: float32 [2048], P('shard')
- grad_mlp_gain: float32 [2048], P('shard')
- grad_query: float32 [2048, 2048], P('shard')
- grad_key: float32 [2048, 2048], P('shard')
- grad_value: float32 [2048, 2048], P('shard')
- grad_output: float32 [2048, 2048], P('shard')
- grad_router: float32 [2048, 16], P('shard')
- grad_gate: float32 [16, 2048, 1024], P(('expert', 'shard'), 'dp')
- grad_up: float32 [16, 2048, 1024], P(('expert', 'shard'), 'dp')
- grad_down: float32 [16, 1024, 2048], P(('expert', 'shard'), None, 'dp')
The draws below stay inside these ranges and needn't reach their ends.
Inputs may be any that keep to these rules, and one draw needn't show every extreme that they name: `doc_lengths`: each row holds a document, then one of 576 tokens, then another document, then the padding; the lengths of a row sum to 768; the first document has 48 to 96 tokens and the padding 192//16 to 24. `expert_ids`: each token names 8 different experts; among the 192 tokens of one device no expert is named more than 120 times, a bound that some block reaches.
All inputs are finite; a program needn't handle non-finite values.
Results may differ from the reference program's by a relative error of at most 0.024.
Values may be sent and summed in bfloat16 or wider, within the bound.
No kernel may reach another device: no remote copies, remote signals or barrier semaphores. Data moves between devices by JAX's collectives and lax.ppermute only.
A program may use at most 320 MiB of HBM per device.

```python
import math
import jax
import jax.numpy as jnp
import numpy as np
from jax import lax

D = 2048
HEADS = 16
HD = 128
FF = 1024
TOP = 8
TOK_DEV = 192
DOCS = 4
EXPERTS = 16
SEQ_LEN = 768
SEQS = 8
TOKENS = 6144
CAP = 120
DOC_MAX = 576


def draw_doc_lengths(key, part):
    key = jax.random.fold_in(key, 11)
    pad_key, open_key = jax.random.split(key)
    padding = jax.random.randint(pad_key, (SEQS, 1), TOK_DEV // 16, TOK_DEV // 8 + 1, dtype=jnp.int32)
    opening = jax.random.randint(open_key, (SEQS, 1), TOK_DEV // 4, TOK_DEV // 2 + 1, dtype=jnp.int32)
    longest = jnp.full((SEQS, 1), DOC_MAX, dtype=jnp.int32)
    closing = (SEQ_LEN - DOC_MAX - padding - opening).astype(jnp.int32)
    return jnp.concatenate([opening, longest, closing, padding], axis=1).astype(jnp.int32)


def level_of(own_key, extent, cuts, low, high):
    loudness = 1.0
    for axis_at, parts in cuts:
        draws = jax.random.uniform(jax.random.fold_in(jax.random.fold_in(own_key, 6), axis_at), (parts,), jnp.float32, low / len(cuts), high / len(cuts))
        loudness = loudness * jnp.repeat(jnp.exp(draws), extent[axis_at] // parts).reshape((-1,) + (1,) * (len(extent) - 1 - axis_at))
    return loudness


def routed_block(key, own, number, rows, count, top, limit, slope):
    order = jax.random.permutation(key, count)
    heavy_load, ordinary = portions_of(count, rows * top, limit, slope, True), portions_of(count, rows * top, limit, slope, False)
    places = jnp.arange(count)

    def named(sizes, rotation):
        used = int((sizes > 0).sum())
        fixed = max(1, used // 4)
        moved = fixed + (places - fixed + rotation * (used - fixed)) % max(1, count - fixed)
        return jnp.zeros((count,), jnp.int32).at[order[jnp.where(places < fixed, places, moved)]].set(jnp.asarray(sizes, jnp.int32))

    sizes = jnp.where(number % 4 == 0, named(heavy_load, number // 4), named(ordinary, number - number // 4 - 1))
    mixed = jax.random.permutation(jax.random.fold_in(own, 3), count)
    source_of, sink = mixed[0:count // 2 * 2:2], mixed[1:count // 2 * 2:2]
    margin = jnp.minimum(sizes[source_of] - 1, limit - sizes[sink]) // 2
    margin = jnp.where((source_of == order[0]) | (sink == order[0]) | (sizes[sink] == 0), 0, jnp.maximum(margin, 0))
    moved = jax.random.randint(jax.random.fold_in(own, 4), (count // 2,), 0, 1 << 20) % (margin + 1)
    sizes = sizes.at[source_of].add(-moved).at[sink].add(moved)
    items = jnp.searchsorted(jnp.cumsum(sizes), jnp.arange(rows * top), side="right").astype(jnp.int32)
    listing = items.reshape(top, rows).T
    listing = listing[jax.random.permutation(jax.random.fold_in(own, 1), rows)]
    rotation = jax.random.randint(jax.random.fold_in(own, 2), (rows, 1), 0, top)
    return jnp.take_along_axis(listing, (jnp.arange(top)[None, :] + rotation) % top, axis=1)


def portions_of(number_of, total, bound, slope, full):
    portions = [(1 << 20) // math.isqrt(grade ** slope) + 1 for grade in range(1, number_of + 1)]
    largest = bound if full else min(bound, max(-(-total // number_of), total * portions[0] // sum(portions)))
    least = 1 if total - largest >= number_of - 1 else 0
    counts, surplus = [largest] + [least] * (number_of - 1), total - largest - least * (number_of - 1)
    while surplus > 0:
        free = [i for i in range(1, number_of) if counts[i] < largest] or [i for i in range(1, number_of) if counts[i] < bound]
        whole, budget = sum([portions[i] for i in free]), surplus
        for i in free:
            extra = min(bound - counts[i], max(1, budget * portions[i] // whole), surplus)
            counts[i] = counts[i] + extra
            surplus = surplus - extra
    return np.array(counts)


def normal_values(rng, dims, deviation, most, cuts=(), held_as=jnp.bfloat16):
    values = jax.random.normal(rng, dims, jnp.float32) * deviation
    if len(cuts) > 0:
        values = level_of(rng, dims, cuts, -0.22, 0.18) * values
    return jnp.clip(values, min=-most, max=most).astype(held_as)


def setup_inputs(seed: int = 0) -> dict:
    seeds = jax.random.split(jax.random.key(seed), 17)
    hidden_in = normal_values(seeds[0], (TOKENS, D), 1.0, 6.0, ((0, 32),))
    grad_out = normal_values(seeds[1], (TOKENS, D), 1.0, 6.0, ((0, 32),))
    doc_lengths = draw_doc_lengths(jax.random.fold_in(seeds[16], 71), 0)
    expert_ids_keys = jax.random.split(jax.random.fold_in(seeds[3], 1), TOKENS // TOK_DEV)
    expert_ids_turns = jax.random.permutation(jax.random.fold_in(seeds[3], 3), TOKENS // TOK_DEV)
    expert_ids = jax.vmap(lambda own, number: routed_block(jax.random.fold_in(seeds[3], 2), own, number, TOK_DEV, EXPERTS, TOP, CAP, 1))(expert_ids_keys, expert_ids_turns).reshape((TOKENS, TOP))
    attn_gain = jnp.clip(1.0 + 0.18 * jax.random.normal(seeds[4], (D,), jnp.float32), 0.099609375, 1.8984375).astype(jnp.bfloat16)
    query_gain = jnp.clip(1.0 + 0.18 * jax.random.normal(seeds[5], (D,), jnp.float32), 0.099609375, 1.8984375).astype(jnp.bfloat16)
    key_gain = jnp.clip(1.0 + 0.18 * jax.random.normal(seeds[6], (D,), jnp.float32), 0.099609375, 1.8984375).astype(jnp.bfloat16)
    mlp_gain = jnp.clip(1.0 + 0.18 * jax.random.normal(seeds[7], (D,), jnp.float32), 0.099609375, 1.8984375).astype(jnp.bfloat16)
    w_query = normal_values(seeds[8], (D, D), D ** -0.5, 0.125, ((0, 4),))
    w_key = normal_values(seeds[9], (D, D), D ** -0.5, 0.125, ((0, 4),))
    w_value = normal_values(seeds[10], (D, D), D ** -0.5, 0.125, ((0, 4),))
    w_output = normal_values(seeds[11], (D, D), (D // 32) ** -0.5, 0.75, ((0, 4),))
    w_router = normal_values(seeds[12], (D, EXPERTS), (4 * D) ** -0.5, 0.0625, ((0, 4),))
    w_gate = normal_values(seeds[13], (EXPERTS, D, FF), D ** -0.5, 0.125, ((0, 16), (1, 2)))
    w_up = normal_values(seeds[14], (EXPERTS, D, FF), D ** -0.5, 0.125, ((0, 16), (1, 2)))
    w_down = normal_values(seeds[15], (EXPERTS, FF, D), (max(1, FF * TOP // (EXPERTS * EXPERTS))) ** -0.5, 1.0, ((0, 16), (2, 2)))
    return dict(hidden_in=hidden_in, grad_out=grad_out, doc_lengths=doc_lengths, expert_ids=expert_ids, attn_gain=attn_gain, query_gain=query_gain, key_gain=key_gain, mlp_gain=mlp_gain, w_query=w_query, w_key=w_key, w_value=w_value, w_output=w_output, w_router=w_router, w_gate=w_gate, w_up=w_up, w_down=w_down)


EPSILON = 1e-05
ROPE_BASE = 10000.0
NEG_FILL = -1e+30
PRECISE = lax.Precision.HIGHEST

@jax.custom_vjp
def low(v):
    return lax.optimization_barrier(v.astype(jnp.bfloat16)).astype(jnp.float32)

@jax.custom_vjp
def low_back(v):
    return v

def low_keep(v):
    return (low(v), None)

def low_pass(kept, grad):
    return (grad,)

def back_keep(v):
    return (v, None)

def back_low(kept, grad):
    return (low(grad),)
low.defvjp(low_keep, low_pass)
low_back.defvjp(back_keep, back_low)

def rms(values, scale_gain):
    return values * lax.rsqrt(lax.optimization_barrier(jnp.mean(values * values, axis=-1, keepdims=True)) + EPSILON) * scale_gain

def softmax_rows(values):
    row_max = lax.optimization_barrier(jnp.max(values, axis=-1, keepdims=True))
    exp_terms = jnp.exp(values - row_max)
    return exp_terms / lax.optimization_barrier(jnp.sum(exp_terms, axis=-1, keepdims=True))

def doc_layout(doc_lengths):
    doc_ends = jnp.cumsum(doc_lengths, axis=1).astype(jnp.int32)
    doc_starts = doc_ends - doc_lengths
    places = jnp.arange(SEQ_LEN, dtype=jnp.int32)
    doc_ids = lax.optimization_barrier(jnp.sum((places[None, :, None] >= doc_ends[:, None, :]).astype(jnp.int32), axis=2)).astype(jnp.int32)
    owner = doc_ids[:, :, None] == jnp.arange(DOCS, dtype=jnp.int32)[None, None, :]
    begins = lax.optimization_barrier(jnp.sum(jnp.where(owner, doc_starts[:, None, :], 0), axis=2)).astype(jnp.int32)
    return (doc_ids, places[None, :] - begins)

def allowed_mask(doc_ids):
    places = jnp.arange(SEQ_LEN, dtype=jnp.int32)
    same_doc = doc_ids[..., :, None] == doc_ids[..., None, :]
    causal = places[None, :] <= places[:, None]
    real_key = doc_ids[..., None, :] < DOCS - 1
    diagonal = places[:, None] == places[None, :]
    return same_doc & causal & (real_key | diagonal)

def rope_tables(doc_place):
    half_size = HD // 2
    freqs = jnp.exp(-math.log(ROPE_BASE) * 2.0 * jnp.arange(half_size, dtype=jnp.float32) / HD)
    angles = doc_place.astype(jnp.float32)[..., None] * freqs
    angles = jnp.concatenate([angles, angles], axis=-1)
    return (jnp.cos(angles), jnp.sin(angles))

def rotate(values, cosine, sine_part):
    half_size = HD // 2
    turned = jnp.concatenate([-values[..., half_size:], values[..., :half_size]], axis=-1)
    return values * cosine[..., None, :] + turned * sine_part[..., None, :]

def expert_table(expert_ids):
    flat_ids = expert_ids.reshape(-1)
    pairs = flat_ids.shape[0]
    expert_hits = (flat_ids[:, None] == jnp.arange(EXPERTS, dtype=jnp.int32)[None, :]).astype(jnp.int32)
    slot_place = (lax.optimization_barrier(jnp.sum(expert_hits * jnp.cumsum(expert_hits, axis=0), axis=1)) - 1).astype(jnp.int32)
    table = jnp.full((EXPERTS, TOKENS // TOK_DEV * CAP), pairs, dtype=jnp.int32)
    return table.at[flat_ids, slot_place].set(jnp.arange(pairs, dtype=jnp.int32))

def attend(block):
    query_blk, key_blk, value_blk, mask_blk = block
    raw_scores = jnp.einsum('gqhd,gkhd->ghqk', query_blk, key_blk, precision=PRECISE) * HD ** (-0.5)
    raw_scores = low_back(raw_scores)
    attn_probs = softmax_rows(jnp.where(mask_blk[:, None], raw_scores, NEG_FILL))
    return jnp.einsum('ghqk,gkhd->gqhd', low(attn_probs), value_blk, precision=PRECISE)

def forward(inputs, gain_attn, gain_query, gain_key, gain_mlp, query_full, key_full, value_full, output_full, router_full, gate_full, up_full, down_full, cosine, sine_part, masks, table, choose):
    count = inputs.shape[0]
    attn_input = low(rms(inputs, gain_attn))
    query_raw = low_back(jnp.dot(attn_input, query_full, precision=PRECISE))
    key_raw = low_back(jnp.dot(attn_input, key_full, precision=PRECISE))
    value_raw = low_back(low(jnp.dot(attn_input, value_full, precision=PRECISE)))
    query_rot = low(rotate(rms(query_raw, gain_query).reshape(count, HEADS, HD), cosine, sine_part))
    key_rot = low(rotate(rms(key_raw, gain_key).reshape(count, HEADS, HD), cosine, sine_part))
    group = math.gcd(SEQS, 4)
    shape = (SEQS // group, group, SEQ_LEN, HEADS, HD)
    mixed = lax.map(jax.checkpoint(attend), (query_rot.reshape(shape), key_rot.reshape(shape), value_raw.reshape(shape), masks.reshape(SEQS // group, group, SEQ_LEN, SEQ_LEN)))
    mixed = low_back(low(mixed.reshape(count, HEADS * HD)))
    residual = inputs + low_back(jnp.dot(mixed, output_full, precision=PRECISE))
    mlp_input = low(rms(residual, gain_mlp))
    logits = low_back(jnp.dot(mlp_input, router_full, precision=PRECISE))
    route_probs = softmax_rows(logits)
    gates = jnp.einsum('tke,te->tk', choose, route_probs, precision=PRECISE)
    padded = jnp.concatenate([mlp_input, jnp.zeros_like(mlp_input[:1])], axis=0)
    gate_list = jnp.concatenate([gates.reshape(-1), jnp.zeros_like(gates[0, :1])], axis=0)

    def one_expert(running, item):
        slot_pairs, weight_gate, weight_up, weight_down = item
        token_of = slot_pairs // TOP
        slot_rows = low_back(padded[token_of])
        gate_pre = low_back(jnp.dot(slot_rows, weight_gate, precision=PRECISE))
        up_pre = low_back(jnp.dot(slot_rows, weight_up, precision=PRECISE))
        hidden_mid = low(gate_pre * jax.nn.sigmoid(gate_pre) * up_pre)
        result = low_back(low(jnp.dot(hidden_mid, weight_down, precision=PRECISE)))
        return (running.at[token_of].add(gate_list[slot_pairs][:, None] * result), None)
    expert_sum, _ = lax.scan(jax.checkpoint(one_expert), jnp.zeros_like(padded), (table, gate_full, up_full, down_full))
    return residual + expert_sum[:count]

def reference(hidden_in, grad_out, doc_lengths, expert_ids, attn_gain, query_gain, key_gain, mlp_gain, w_query, w_key, w_value, w_output, w_router, w_gate, w_up, w_down):
    doc_ids, doc_place = doc_layout(doc_lengths)
    cosine, sine_part = rope_tables(doc_place.reshape(-1))
    masks = allowed_mask(doc_ids)
    choose = (expert_ids[:, :, None] == jnp.arange(EXPERTS, dtype=jnp.int32)[None, None, :]).astype(jnp.float32)
    table = expert_table(expert_ids)
    params = tuple((item.astype(jnp.float32) for item in (hidden_in, attn_gain, query_gain, key_gain, mlp_gain, w_query, w_key, w_value, w_output, w_router, w_gate, w_up, w_down)))

    def run(*values):
        return forward(*values, cosine, sine_part, masks, table, choose)
    result, pull = jax.vjp(run, *params)
    grads = pull(grad_out.astype(jnp.float32))
    return (result.astype(jnp.bfloat16), grads[0], grads[1], grads[2], grads[3], grads[4], grads[5], grads[6], grads[7], grads[8], grads[9], grads[10], grads[11], grads[12])
```

```python
import math

import jax
import jax.numpy as jnp
from jax import lax
from jax.sharding import PartitionSpec as P

D = 2048
HEADS = 16
HD = 128
TOP = 8
DOCS = 4

EPSILON = 1e-05
ROPE_BASE = 10000.0
NEG_FILL = -1e30

F32 = jnp.float32
BF16 = jnp.bfloat16


def dot(a, b):
    return jnp.dot(a, b, preferred_element_type=F32)


def dot_nt(a, b):
    return lax.dot_general(a, b, (((1,), (1,)), ((), ())), preferred_element_type=F32)


def dot_tn(a, b):
    return lax.dot_general(a, b, (((0,), (0,)), ((), ())), preferred_element_type=F32)


def at(stack, index):
    return lax.dynamic_index_in_dim(stack, index, 0, keepdims=False)


def doc_layout(lengths, total):
    doc_ends = jnp.cumsum(lengths)
    doc_starts = doc_ends - lengths
    places = jnp.arange(total, dtype=jnp.int32)
    doc_ids = jnp.sum((places[:, None] >= doc_ends[None, :]).astype(jnp.int32), axis=1)
    owner = doc_ids[:, None] == jnp.arange(DOCS, dtype=jnp.int32)[None, :]
    begins = jnp.sum(jnp.where(owner, doc_starts[None, :], 0), axis=1)
    return doc_ids, places - begins


def rope_tables(doc_place):
    half_size = HD // 2
    freqs = jnp.exp(-math.log(ROPE_BASE) * 2.0 * jnp.arange(half_size, dtype=F32) / HD)
    angles = doc_place.astype(F32)[:, None] * freqs
    angles = jnp.concatenate([angles, angles], axis=-1)
    return jnp.cos(angles), jnp.sin(angles)


def turn(values):
    half_size = HD // 2
    return jnp.concatenate([-values[..., half_size:], values[..., :half_size]], axis=-1)


def turn_back(values):
    half_size = HD // 2
    return jnp.concatenate([values[..., half_size:], -values[..., :half_size]], axis=-1)


def shards(
    hidden_in,
    grad_out,
    doc_lengths,
    expert_ids,
    attn_gain,
    query_gain,
    key_gain,
    mlp_gain,
    w_query,
    w_key,
    w_value,
    w_output,
    w_router,
    w_gate,
    w_up,
    w_down,
):
    length = hidden_in.shape[0]
    members = lax.axis_size("shard")
    planes = lax.axis_size("expert")
    me = lax.axis_index("shard")
    mz = lax.axis_index("expert")
    md = lax.axis_index("dp")
    total = length * members
    experts = planes * members
    capacity = 5 * length * TOP // (4 * experts)
    own = D // members
    local_heads = HEADS // members
    scale = HD ** (-0.5)
    others = range(1, members)

    def swap(value, k):
        return lax.ppermute(value, "shard", [(i, i ^ k) for i in range(members)])

    def fetch_z(value, j):
        return lax.ppermute(value, "expert", [(i, (i - j) % planes) for i in range(planes)])

    def return_z(value, j):
        return lax.ppermute(value, "expert", [(i, (i + j) % planes) for i in range(planes)])

    def swap_dp(value):
        return lax.ppermute(value, "dp", [(0, 1), (1, 0)])

    def plane_gather(value):
        relative = jnp.stack([value] + [swap(value, k) for k in others])
        return jnp.concatenate([at(relative, me ^ j) for j in range(members)], axis=0)

    def plane_sum(value):
        result = value
        for k in others:
            result = result + swap(value, k)
        return result

    def plane_scatter(partial, rows):
        pieces = partial.reshape(members, rows, partial.shape[1])
        result = at(pieces, me)
        low = pieces.astype(BF16)
        for k in others:
            result = result + swap(at(low, me ^ k), k).astype(F32)
        return result

    def order_z(values):
        stack = jnp.stack(values)
        return [at(stack, (z - mz) % planes) for z in range(planes)]

    small = jnp.concatenate([w_router.T, attn_gain[None], mlp_gain[None]], axis=0)
    small_all = jnp.stack([small] + [swap(small, k) for k in others])
    small_all = jnp.concatenate([at(small_all, me ^ j) for j in range(members)], axis=1)
    router_t = small_all[:experts]
    gain_attn = small_all[experts].astype(F32)
    gain_mlp = small_all[experts + 1].astype(F32)
    gain_query = query_gain.astype(F32)
    gain_key = key_gain.astype(F32)

    hidden_all = plane_gather(hidden_in).astype(F32)

    half = own // 2

    def column_blocks(dest):
        return jnp.concatenate(
            [lax.dynamic_slice_in_dim(w, dest * own, own, 1) for w in (w_query, w_key, w_value)],
            axis=1,
        )

    got = []
    for k in others:
        block = column_blocks(me ^ k)
        got.append(swap(lax.dynamic_slice_in_dim(block, md * half, half, 0), k))
    got = jnp.stack(got)
    peer = swap_dp(got)
    first = jnp.where(md == 0, got, peer)
    second = jnp.where(md == 0, peer, got)
    blocks = jnp.concatenate([first, second], axis=1)
    blocks = jnp.concatenate([column_blocks(me)[None], blocks], axis=0)
    w_qkv = jnp.concatenate([at(blocks, me ^ j) for j in range(members)], axis=0)

    doc_ids, doc_place = doc_layout(doc_lengths[0], total)
    cosine, sine = rope_tables(doc_place)
    cosine, sine = cosine[:, None, :], sine[:, None, :]
    places = jnp.arange(total, dtype=jnp.int32)
    allowed = (
        (doc_ids[:, None] == doc_ids[None, :])
        & (places[None, :] <= places[:, None])
        & ((doc_ids[None, :] < DOCS - 1) | (places[None, :] == places[:, None]))
    )[None]

    ids_z = [expert_ids] + [fetch_z(expert_ids, j) for j in range(1, planes)]
    plane_experts = mz * members + jnp.arange(members, dtype=jnp.int32)
    slot_axis = jnp.arange(capacity, dtype=jnp.int32)

    def slots_of(ids):
        hit = jnp.any(ids[:, :, None] == plane_experts[None, None, :], axis=1)
        rank = jnp.cumsum(hit.astype(jnp.int32), axis=0) - 1
        place = jnp.where(hit, rank, -1).T
        return place[:, None, :] == slot_axis[None, :, None]

    picks = [slots_of(ids) for ids in ids_z]
    picks_low = [p.astype(BF16) for p in picks]

    def dispatch(blocks_z):
        received = []
        for j in range(planes):
            rows = lax.dot_general(
                picks_low[j], blocks_z[j], (((2,), (0,)), ((), ())), preferred_element_type=F32
            ).astype(BF16)
            received.append(
                jnp.stack([at(rows, me)] + [swap(at(rows, me ^ k), k) for k in others])
            )
        return jnp.stack(received).reshape(planes * members * capacity, D)

    def collect(rows):
        rows = rows.reshape(planes, members, capacity, D)
        sums = []
        for j in range(planes):
            relative = [rows[j, 0]] + [swap(rows[j, k], k) for k in others]
            relative = jnp.stack(relative)
            expert_rows = jnp.concatenate([at(relative, me ^ s) for s in range(members)], axis=0)
            pick = picks_low[j].reshape(members * capacity, length)
            sums.append(dot_tn(pick, expert_rows))
        result = sums[0]
        for j in range(1, planes):
            result = result + return_z(sums[j].astype(BF16), j).astype(F32)
        return result

    def whole(weight, axis):
        mine = weight[0]
        peer_half = swap_dp(mine)
        low_half = jnp.where(md == 0, mine, peer_half)
        high_half = jnp.where(md == 0, peer_half, mine)
        return jnp.concatenate([low_half, high_half], axis=axis)

    gate_full = whole(w_gate, 0)
    up_full = whole(w_up, 0)
    down_full = whole(w_down, 1)

    inv_in = lax.rsqrt(jnp.mean(hidden_all * hidden_all, axis=-1, keepdims=True) + EPSILON)
    attn_input = (hidden_all * inv_in * gain_attn).astype(BF16)
    raw = dot(attn_input, w_qkv)
    query_raw = raw[:, :own]
    key_raw = raw[:, own : 2 * own]
    value_rows = raw[:, 2 * own :].astype(BF16)
    squares = jnp.stack([jnp.sum(query_raw * query_raw, axis=-1), jnp.sum(key_raw * key_raw, axis=-1)])
    squares = plane_sum(squares)
    inverse = lax.rsqrt(squares / D + EPSILON)
    inv_query, inv_key = inverse[0][:, None], inverse[1][:, None]

    def to_heads(rows):
        return rows.reshape(total, local_heads, HD)

    def rope(rows):
        v = to_heads(rows)
        return v * cosine + turn(v) * sine

    query_heads = rope(query_raw * inv_query * gain_query).astype(BF16)
    key_heads = rope(key_raw * inv_key * gain_key).astype(BF16)
    value_heads = to_heads(value_rows)
    scores = jnp.einsum("qhd,khd->hqk", query_heads, key_heads, preferred_element_type=F32) * scale
    scores = jnp.where(allowed, scores, NEG_FILL)
    row_max = jnp.max(scores, axis=-1, keepdims=True)
    exp_terms = jnp.exp(scores - row_max)
    probs = exp_terms / jnp.sum(exp_terms, axis=-1, keepdims=True)
    probs_low = probs.astype(BF16)
    mixed = jnp.einsum("hqk,khd->qhd", probs_low, value_heads, preferred_element_type=F32)
    mixed = mixed.astype(BF16).reshape(total, own)
    residual = hidden_in.astype(F32) + plane_scatter(dot(mixed, w_output), length)

    inv_mlp = lax.rsqrt(jnp.mean(residual * residual, axis=-1, keepdims=True) + EPSILON)
    unit_mlp = residual * inv_mlp
    mlp_input = (unit_mlp * gain_mlp).astype(BF16)
    logits = dot_nt(mlp_input, router_t)
    top_logit = jnp.max(logits, axis=-1, keepdims=True)
    exp_logits = jnp.exp(logits - top_logit)
    route = exp_logits / jnp.sum(exp_logits, axis=-1, keepdims=True)

    input_z = [mlp_input] + [fetch_z(mlp_input, j) for j in range(1, planes)]
    route_z = [route] + [fetch_z(route, j) for j in range(1, planes)]
    grads_z = [grad_out] + [fetch_z(grad_out, j) for j in range(1, planes)]
    gate_parts = []
    for j in range(planes):
        local_route = lax.dynamic_slice_in_dim(route_z[j], mz * members, members, 1).T
        gate_parts.append(jnp.sum(jnp.where(picks[j], local_route[:, None, :], 0.0), axis=-1))
    gate_slots = jnp.stack(gate_parts, axis=1)
    gate_rows = jnp.stack(
        [at(gate_slots, me)] + [swap(at(gate_slots, me ^ k), k) for k in others], axis=1
    ).reshape(planes * members * capacity)[:, None]
    slot_rows = dispatch(input_z)
    slot_grads = dispatch(grads_z)

    gate_pre = dot(slot_rows, gate_full)
    up_pre = dot(slot_rows, up_full)
    sig = jax.nn.sigmoid(gate_pre)
    silu = gate_pre * sig
    middle = (silu * up_pre).astype(BF16)
    raw_grad = dot_nt(slot_grads, down_full)
    gate_grad = jnp.sum(raw_grad * middle.astype(F32), axis=-1)
    grad_middle = raw_grad * gate_rows
    grad_gate_pre = (grad_middle * up_pre * sig * (1.0 + gate_pre * (1.0 - sig))).astype(BF16)
    grad_up_pre = (grad_middle * silu).astype(BF16)
    grad_rows = (dot_nt(grad_gate_pre, gate_full) + dot_nt(grad_up_pre, up_full)).astype(BF16)
    grad_mlp_in = collect(grad_rows)
    weighted = (dot(middle, down_full) * gate_rows).astype(BF16)
    block_out = (residual + collect(weighted)).astype(BF16)
    slot_dy = (slot_grads.astype(F32) * gate_rows).astype(BF16)
    grad_down_full = dot_tn(middle, slot_dy)
    grad_gate_full = dot_tn(slot_rows, grad_gate_pre)
    grad_up_full = dot_tn(slot_rows, grad_up_pre)

    def halves_sum(full, axis):
        size = full.shape[axis] // 2
        mine = lax.dynamic_slice_in_dim(full, md * size, size, axis)
        away = lax.dynamic_slice_in_dim(full, (1 - md) * size, size, axis)
        return mine + swap_dp(away.astype(BF16)).astype(F32)

    grad_gate = halves_sum(grad_gate_full, 0)[None]
    grad_up = halves_sum(grad_up_full, 0)[None]
    grad_down = halves_sum(grad_down_full, 1)[None]

    gate_grad = gate_grad.reshape(planes, members, capacity)
    relative = jnp.stack([gate_grad[:, 0]] + [swap(gate_grad[:, k], k) for k in others])
    by_expert = jnp.stack([at(relative, me ^ s) for s in range(members)])
    parts = []
    for j in range(planes):
        parts.append(jnp.sum(jnp.where(picks[j], by_expert[:, j, :, None], 0.0), axis=1))
    parts = [parts[0]] + [return_z(parts[j], j) for j in range(1, planes)]
    parts = jnp.stack(parts)
    grad_route = jnp.concatenate([at(parts, (mz - z) % planes) for z in range(planes)], axis=0).T
    grad_logits = (
        route * (grad_route - jnp.sum(route * grad_route, axis=-1, keepdims=True))
    ).astype(BF16)
    grad_mlp_in = grad_mlp_in + dot(grad_logits, router_t)
    grad_router_part = dot_tn(grad_logits, mlp_input)
    grad_gain_mlp_part = jnp.sum(grad_mlp_in * unit_mlp, axis=0)
    upstream = grad_out.astype(F32)
    scaled = grad_mlp_in * gain_mlp
    grad_residual = (
        upstream
        + (scaled - unit_mlp * jnp.mean(scaled * unit_mlp, axis=-1, keepdims=True)) * inv_mlp
    )
    grad_attn_all = plane_gather(grad_residual.astype(BF16))

    grad_output_part = dot_tn(mixed, grad_attn_all)
    grad_mixed = to_heads(dot_nt(grad_attn_all, w_output).astype(BF16))
    grad_value = jnp.einsum("hqk,qhd->khd", probs_low, grad_mixed, preferred_element_type=F32)
    grad_probs = jnp.einsum("qhd,khd->hqk", grad_mixed, value_heads, preferred_element_type=F32)
    row_delta = jnp.sum(probs * grad_probs, axis=-1, keepdims=True)
    grad_scores = (probs * (grad_probs - row_delta)).astype(BF16)
    grad_query_rot = (
        jnp.einsum("hqk,khd->qhd", grad_scores, key_heads, preferred_element_type=F32) * scale
    )
    grad_key_rot = (
        jnp.einsum("hqk,qhd->khd", grad_scores, query_heads, preferred_element_type=F32) * scale
    )

    def unrope(rows):
        return (rows * cosine + turn_back(rows * sine)).reshape(total, own)

    grad_query_normed = unrope(grad_query_rot)
    grad_key_normed = unrope(grad_key_rot)
    unit_query = query_raw * inv_query
    unit_key = key_raw * inv_key
    grad_gain_query = jnp.sum(grad_query_normed * unit_query, axis=0)
    grad_gain_key = jnp.sum(grad_key_normed * unit_key, axis=0)
    scaled_query = grad_query_normed * gain_query
    scaled_key = grad_key_normed * gain_key
    means = jnp.stack(
        [jnp.sum(scaled_query * unit_query, axis=-1), jnp.sum(scaled_key * unit_key, axis=-1)]
    )
    means = plane_sum(means) / D
    grad_query_low = ((scaled_query - unit_query * means[0][:, None]) * inv_query).astype(BF16)
    grad_key_low = ((scaled_key - unit_key * means[1][:, None]) * inv_key).astype(BF16)
    grad_value_low = grad_value.astype(BF16).reshape(total, own)
    grad_raw = jnp.concatenate([grad_query_low, grad_key_low, grad_value_low], axis=1)
    grad_attn_in = plane_scatter(dot_nt(grad_raw, w_qkv), length)
    inputs = hidden_in.astype(F32)
    inv_own = lax.rsqrt(jnp.mean(inputs * inputs, axis=-1, keepdims=True) + EPSILON)
    unit_in = inputs * inv_own
    grad_gain_attn_part = jnp.sum(grad_attn_in * unit_in, axis=0)
    scaled_in = grad_attn_in * gain_attn
    grad_in = (
        grad_residual
        + (scaled_in - unit_in * jnp.mean(scaled_in * unit_in, axis=-1, keepdims=True)) * inv_own
    )

    grad_qkv = dot_tn(attn_input, grad_raw)
    slab = half // planes

    def scatter_sum(pieces):
        mine = at(pieces, md)
        mine = mine + swap_dp(at(pieces, 1 - md).astype(BF16)).astype(F32)
        result = at(mine, mz)
        low = mine.astype(BF16)
        for j in range(1, planes):
            result = result + return_z(at(low, (mz + j) % planes), j).astype(F32)
        return result

    def gather_back(piece):
        every = jnp.stack(order_z([piece] + [fetch_z(piece, j) for j in range(1, planes)]))
        peer_side = swap_dp(every)
        return jnp.stack([jnp.where(md == 0, every, peer_side), jnp.where(md == 0, peer_side, every)])

    pieces = grad_qkv.reshape(members, 2, planes, slab, 3 * own).transpose(1, 2, 0, 3, 4)
    piece = scatter_sum(pieces).astype(BF16)
    relative = jnp.stack([at(piece, me)] + [swap(at(piece, me ^ k), k) for k in others])
    piece = jnp.stack([at(relative, me ^ s) for s in range(members)])
    full = gather_back(piece)
    full = full.reshape(2, planes, members, slab, 3, own).transpose(4, 0, 1, 3, 2, 5)
    full = full.reshape(3, own, D).astype(F32)
    grad_query, grad_key, grad_value_w = full[0], full[1], full[2]

    piece = scatter_sum(grad_output_part.reshape(2, planes, slab, D)).astype(BF16)
    grad_output = gather_back(piece).reshape(own, D).astype(F32)

    small_part = jnp.concatenate(
        [grad_router_part, grad_gain_attn_part[None], grad_gain_mlp_part[None]], axis=0
    )
    small_pieces = small_part.reshape(experts + 2, members, own).transpose(1, 0, 2)
    small_sum = at(small_pieces, me)
    for k in others:
        small_sum = small_sum + swap(at(small_pieces, me ^ k), k)
    small_sum = jnp.concatenate([small_sum, grad_gain_query[None], grad_gain_key[None]], axis=0)
    small_sum = small_sum + swap_dp(small_sum)
    small_sum = order_z([small_sum] + [fetch_z(small_sum, j) for j in range(1, planes)])
    small_total = small_sum[0]
    for z in range(1, planes):
        small_total = small_total + small_sum[z]
    return (
        block_out,
        grad_in,
        small_total[experts],
        small_total[experts + 2],
        small_total[experts + 3],
        small_total[experts + 1],
        grad_query,
        grad_key,
        grad_value_w,
        grad_output,
        small_total[:experts].T,
        grad_gate,
        grad_up,
        grad_down,
    )


def solution(mesh):
    return jax.shard_map(
        shards,
        mesh=mesh,
        in_specs=(
            P(("dp", "expert", "shard"), None),
            P(("dp", "expert", "shard"), None),
            P(("dp", "expert"), None),
            P(("dp", "expert", "shard"), None),
            P("shard"),
            P("shard"),
            P("shard"),
            P("shard"),
            P("shard", None),
            P("shard", None),
            P("shard", None),
            P("shard", None),
            P("shard", None),
            P(("expert", "shard"), "dp", None),
            P(("expert", "shard"), "dp", None),
            P(("expert", "shard"), None, "dp"),
        ),
        out_specs=(
            P(("dp", "expert", "shard"), None),
            P(("dp", "expert", "shard"), None),
            P("shard"),
            P("shard"),
            P("shard"),
            P("shard"),
            P("shard", None),
            P("shard", None),
            P("shard", None),
            P("shard", None),
            P("shard", None),
            P(("expert", "shard"), "dp", None),
            P(("expert", "shard"), "dp", None),
            P(("expert", "shard"), None, "dp"),
        ),
        check_vma=False,
    )
```

```python
import functools
import math

import jax
import jax.numpy as jnp
from jax import lax
from jax.experimental import pallas as pl
from jax.experimental.pallas import tpu as pltpu
from jax.sharding import PartitionSpec as P

D = 2048
HEADS = 16
HD = 128
TOP = 8
DOCS = 4

EPSILON = 1e-05
ROPE_BASE = 10000.0
NEG_FILL = -1e30

F32 = jnp.float32
BF16 = jnp.bfloat16


def dot(a, b):
    return jnp.dot(a, b, preferred_element_type=F32)


def dot_nt(a, b):
    return lax.dot_general(a, b, (((1,), (1,)), ((), ())), preferred_element_type=F32)


def dot_tn(a, b):
    return lax.dot_general(a, b, (((0,), (0,)), ((), ())), preferred_element_type=F32)


def at(stack, index):
    return lax.dynamic_index_in_dim(stack, index, 0, keepdims=False)


def doc_layout(lengths, total):
    doc_ends = jnp.cumsum(lengths)
    doc_starts = doc_ends - lengths
    places = jnp.arange(total, dtype=jnp.int32)
    doc_ids = jnp.sum((places[:, None] >= doc_ends[None, :]).astype(jnp.int32), axis=1)
    owner = doc_ids[:, None] == jnp.arange(DOCS, dtype=jnp.int32)[None, :]
    begins = jnp.sum(jnp.where(owner, doc_starts[None, :], 0), axis=1)
    return doc_ids, places - begins


def rope_tables(doc_place):
    half_size = HD // 2
    freqs = jnp.exp(-math.log(ROPE_BASE) * 2.0 * jnp.arange(half_size, dtype=F32) / HD)
    angles = doc_place.astype(F32)[:, None] * freqs
    angles = jnp.concatenate([angles, angles], axis=-1)
    return jnp.cos(angles), jnp.sin(angles)


PART = 256
MIB = 1024 * 1024


def call(body, args, kinds, outs, scratch=(), vmem=40, flops=0, moved=0, after=()):
    spaces = {"v": pltpu.VMEM, "s": pltpu.SMEM, "a": pl.ANY}
    count = len(args)

    def run(*refs):
        body(*refs[:count], *refs[count + len(after) :])

    return pl.pallas_call(
        run,
        out_shape=[jax.ShapeDtypeStruct(shape, dtype) for shape, dtype in outs],
        in_specs=[pl.BlockSpec(memory_space=spaces[kind]) for kind in kinds + "a" * len(after)],
        out_specs=[pl.BlockSpec(memory_space=pltpu.VMEM) for _ in outs],
        scratch_shapes=list(scratch),
        compiler_params=pltpu.CompilerParams(vmem_limit_bytes=vmem * MIB),
        cost_estimate=pl.CostEstimate(flops=flops, bytes_accessed=moved, transcendentals=0),
    )(*args, *after)


def copy_all(pairs, sems):
    copies = [pltpu.make_async_copy(a, b, sems.at[i]) for i, (a, b) in enumerate(pairs)]
    for c in copies:
        c.start()
    for c in copies:
        c.wait()


def iota(shape, axis):
    return lax.broadcasted_iota(jnp.int32, shape, axis)


def split3(x):
    hi = x.astype(BF16).astype(F32)
    mid = (x - hi).astype(BF16).astype(F32)
    lo = (x - hi - mid).astype(BF16).astype(F32)
    return hi, mid, lo


def pick_rows(place, slots):
    return jnp.where(iota((slots, place.shape[1]), 0) == place, 1.0, 0.0).astype(BF16)


def dispatch_body(gated, members, capacity, slots, idx, place, rows, *outs):
    length = place.shape[1]
    me, mz = idx[0], idx[1]
    source = rows[0:length, :]
    for k in range(members):
        expert = mz * members + (me ^ k)
        pick = pick_rows(place[pl.ds(expert, 1), :], slots)
        result = dot(pick, source)
        outs[k][...] = result.astype(BF16)
        if gated:
            experts = place.shape[0]
            head = result[:, 0:128]
            row = iota((slots, 128), 0)
            for part in range(3):
                table = rows[length : length + experts, part * PART : part * PART + length].astype(F32)
                gate = jnp.sum(jnp.where(iota(table.shape, 0) == expert, table, 0.0), axis=0, keepdims=True)
                gate = jnp.broadcast_to(gate, (8, length)).astype(BF16)
                slot = dot_nt(gate, pick)[0:1, :]
                if slots < 128:
                    slot = jnp.concatenate([slot, jnp.zeros((1, 128 - slots), F32)], axis=1)
                head = head + jnp.where(row == capacity + part, slot, 0.0)
            outs[k][:, 0:128] = head.astype(BF16)


def expert_body(members, capacity, slots, first, idx, *refs):
    xs, cs = refs[:members], refs[members : 2 * members]
    ga, gb, ua, ub, da, db = refs[2 * members : 2 * members + 6]
    rest = refs[2 * members + 6 :]
    ds, (gm, dz, du), (x, c, sems) = rest[:members], rest[members : members + 3], rest[members + 3 :]
    pairs = [(xs[k], x.at[pl.ds(k * slots, slots)]) for k in range(members)]
    pairs += [(cs[k].at[pl.ds(first, slots)], c.at[pl.ds(k * slots, slots)]) for k in range(members)]
    copy_all(pairs, sems)
    md = idx[2]
    half = ga.shape[0]
    inner = ga.shape[1]
    mine = pl.ds(pl.multiple_of(md * half, half), half)
    peer = pl.ds(pl.multiple_of((1 - md) * half, half), half)
    rows = members * slots
    eye = iota((slots, 128), 0) == iota((slots, 128), 1)
    row = iota((slots, 128), 0)
    gates = []
    for k in range(members):
        part = x[k * slots : (k + 1) * slots, 0:128].astype(F32)
        line = jnp.sum(
            jnp.where((row >= capacity) & (row < capacity + 3), part, 0.0), axis=0, keepdims=True
        )
        gates.append(jnp.sum(jnp.where(eye, line, 0.0), axis=1, keepdims=True))
    gate = jnp.concatenate(gates, axis=0)
    gate_grad = jnp.zeros((rows, 1), F32)
    step = 512
    for n in range(0, inner, step):
        cols = slice(n, n + step)
        z = dot(x[:, mine], ga[:, cols]) + dot(x[:, peer], gb[:, cols])
        u = dot(x[:, mine], ua[:, cols]) + dot(x[:, peer], ub[:, cols])
        raw = dot_nt(c[:, mine], da[cols, :]) + dot_nt(c[:, peer], db[cols, :])
        sig = 1.0 / (1.0 + jnp.exp(-z))
        silu = z * sig
        middle = silu * u
        gate_grad = gate_grad + jnp.sum(
            raw * middle.astype(BF16).astype(F32), axis=1, keepdims=True
        )
        gm[:, cols] = (gate * middle).astype(BF16)
        raw = raw * gate
        dz[:, cols] = (raw * u * sig * (1.0 + z * (1.0 - sig))).astype(BF16)
        du[:, cols] = (raw * silu).astype(BF16)
    lines = []
    for k in range(members):
        col = gate_grad[k * slots : (k + 1) * slots]
        lines.append(jnp.sum(jnp.where(eye, col, 0.0), axis=0, keepdims=True))
    for part, (wg, wu) in ((mine, (ga, ua)), (peer, (gb, ub))):
        result = dot_nt(dz[...], wg[...]) + dot_nt(du[...], wu[...])
        for k in range(members):
            ds[k][:, part] = result[k * slots : (k + 1) * slots].astype(BF16)
    for k in range(members):
        head = ds[k][:, 0:128].astype(F32)
        for i, value in enumerate(split3(lines[k])):
            head = head + jnp.where(row == capacity + i, value, 0.0)
        ds[k][:, 0:128] = head.astype(BF16)


def collect_body(graded, low, members, capacity, slots, idx, place, *refs):
    rows, outs, (stack, pick, sems) = refs[:members], refs[members:-3], refs[-3:]
    length = place.shape[1]
    me, mz = idx[0], idx[1]
    copies = [
        pltpu.make_async_copy(rows[k], stack.at[pl.ds(k * slots, slots)], sems.at[k])
        for k in range(members)
    ]
    for copy in copies:
        copy.start()
    for k in range(members):
        expert = mz * members + (me ^ k)
        pick[k * slots : (k + 1) * slots, :] = pick_rows(place[pl.ds(expert, 1), :], slots)
    for copy in copies:
        copy.wait()
    out = outs[0]
    result = dot_tn(pick[...], stack[...])
    out[0:length, :] = result.astype(out.dtype)
    if not graded:
        return
    slab = iota((16, length), 0)
    lines = jnp.zeros((16, length), F32)
    row = iota((slots, 128), 0)
    for k in range(members):
        head = stack[k * slots : (k + 1) * slots, 0:128].astype(F32)
        pieces = [
            jnp.sum(jnp.where(row == capacity + i, head, 0.0), axis=0, keepdims=True) for i in range(3)
        ]
        pieces = jnp.concatenate(pieces + [jnp.zeros((5, 128), F32)], axis=0).astype(BF16)
        line = jnp.sum(
            dot(pieces[:, 0:slots], pick[k * slots : (k + 1) * slots, :]), axis=0, keepdims=True
        )
        lines = lines + jnp.where(slab == (me ^ k), line, 0.0)
    if low:
        out[length : length + 16, :] = jnp.zeros((16, out.shape[1]), BF16)
        for i, value in enumerate(split3(lines)):
            out[length : length + 16, i * PART : i * PART + length] = value.astype(BF16)
    else:
        outs[1][...] = lines


def row_grad_body(count, slots, idx, *refs):
    pieces, blocks = refs[: count[0]], refs[count[0] : count[0] + count[1]]
    keep, away, a, b, sems = refs[count[0] + count[1] :]
    size = blocks[0].shape[0]
    pairs = [(p, a.at[pl.ds(i * slots, slots)]) for i, p in enumerate(pieces)]
    pairs += [(q, b.at[pl.ds(i * size, size)]) for i, q in enumerate(blocks)]
    copy_all(pairs, sems)
    md = idx[2]
    half = keep.shape[0]
    step = 256
    for n in range(0, half, step):
        other = pl.multiple_of((1 - md) * half + n, step)
        away[n : n + step, :] = dot_tn(a[:, pl.ds(other, step)], b[...]).astype(BF16)
    for n in range(0, half, step):
        this = pl.multiple_of(md * half + n, step)
        keep[n : n + step, :] = dot_tn(a[:, pl.ds(this, step)], b[...])


def col_grad_body(planes, members, slots, idx, *refs):
    blocks, arrays = refs[:planes], refs[planes:-5]
    keep, away, a, b, sems = refs[-5:]
    size = blocks[0].shape[0]
    pairs = [(q, a.at[pl.ds(i * size, size)]) for i, q in enumerate(blocks)]
    span = arrays[0].shape[0] // slots
    groups = len(arrays) // members
    for g in range(groups):
        for k in range(members):
            for i in range(span):
                at_row = ((g * span + i) * members + k) * slots
                pairs.append((arrays[g * members + k].at[pl.ds(i * slots, slots)], b.at[pl.ds(at_row, slots)]))
    copy_all(pairs, sems)
    md = idx[2]
    half = keep.shape[1]
    step = 256
    for n in range(0, keep.shape[0], step):
        lhs = a[:, n : n + step]
        other = pl.ds(pl.multiple_of((1 - md) * half, half), half)
        away[n : n + step, :] = dot_tn(lhs, b[:, other]).astype(BF16)
    for n in range(0, keep.shape[0], step):
        lhs = a[:, n : n + step]
        this = pl.ds(pl.multiple_of(md * half, half), half)
        keep[n : n + step, :] = dot_tn(lhs, b[:, this])


def down_body(planes, members, slots, idx, *refs):
    blocks, (da, db), outs = refs[:planes], refs[planes : planes + 2], refs[planes + 2 :]
    md = idx[2]
    half = da.shape[1]
    for j in range(planes):
        for part, w in ((md, da), (1 - md, db)):
            cols = pl.ds(pl.multiple_of(part * half, half), half)
            result = dot(blocks[j][...], w[...])
            for k in range(members):
                outs[k][j * slots : (j + 1) * slots, cols] = result[k * slots : (k + 1) * slots].astype(BF16)


def to_row(column):
    eye = iota((128, 128), 0) == iota((128, 128), 1)
    return jnp.concatenate(
        [
            jnp.sum(jnp.where(eye, column[i : i + 128], 0.0), axis=0, keepdims=True)
            for i in range(0, column.shape[0], 128)
        ],
        axis=1,
    )


def to_column(line):
    eye = iota((128, 128), 0) == iota((128, 128), 1)
    return jnp.sum(jnp.where(eye, line, 0.0), axis=1, keepdims=True)


def prepare_body(members, idx, wq, wk, wv, *outs):
    me, md = idx[0], idx[2]
    half = outs[0].shape[0]
    own = wq.shape[1] // members
    rows = pl.ds(pl.multiple_of(md * half, half), half)
    for k in range(1, members):
        cols = pl.ds(pl.multiple_of((me ^ k) * own, own), own)
        for i, w in enumerate((wq, wk, wv)):
            outs[k - 1][:, i * own : (i + 1) * own] = w[rows, cols]


def project_body(members, experts, idx, *refs):
    hs, sms = refs[:members], refs[members : 2 * members]
    refs = refs[2 * members :]
    ws, got, peer = refs[:3], refs[3 : 2 + members], refs[2 + members : 1 + 2 * members]
    q0, k0, v, a, w, squares, gain, sems = refs[1 + 2 * members :]
    me, md = idx[0], idx[2]
    length, total = hs[0].shape[0], a.shape[0]
    own = q0.shape[1]
    half = own // 2
    copies = []
    base = pl.multiple_of(me * own, own)
    for i in range(3):
        copies.append((ws[i].at[:, pl.ds(base, own)], w.at[pl.ds(base, own), i * own : (i + 1) * own]))
    for k in range(1, members):
        for side, source in ((md, got), (1 - md, peer)):
            row = pl.multiple_of((me ^ k) * own + side * half, half)
            copies.append((source[k - 1], w.at[pl.ds(row, half)]))
    copies = [pltpu.make_async_copy(s, d, sems.at[i]) for i, (s, d) in enumerate(copies)]
    for c in copies:
        c.start()
    for k in range(members):
        cols = pl.ds(pl.multiple_of((me ^ k) * own, own), own)
        gain[:, cols] = sms[k][experts : experts + 1, :].astype(F32)
    for k in range(members):
        h = hs[k][...].astype(F32)
        inv = lax.rsqrt(jnp.mean(h * h, axis=-1, keepdims=True) + EPSILON)
        rows = pl.ds(pl.multiple_of((me ^ k) * length, length), length)
        a[rows, :] = (h * inv * gain[...]).astype(BF16)
    for c in copies:
        c.wait()
    step = 256
    sums = [[], []]
    for n in range(0, total, step):
        rows = slice(n, n + step)
        for i, out in enumerate((q0, k0)):
            raw = dot(a[rows, :], w[:, i * own : (i + 1) * own])
            out[rows, :] = raw
            sums[i].append(jnp.sum(raw * raw, axis=1, keepdims=True))
        v[rows, :] = dot(a[rows, :], w[:, 2 * own :]).astype(BF16)
    lines = [to_row(jnp.concatenate(s, axis=0)) for s in sums]
    squares[...] = jnp.concatenate(lines + [jnp.zeros((6, total), F32)], axis=0)


def doc_start(lens, first, count):
    end0 = lens[0, 0]
    end1 = end0 + lens[0, 1]
    end2 = end1 + lens[0, 2]
    at_row = iota((count, 1), 0) + first
    later = jnp.where(at_row < end2, end1, at_row)
    start = jnp.where(at_row < end0, 0, jnp.where(at_row < end1, end0, later))
    return at_row, start


def inverse_rms(squares):
    total = squares[0][...]
    for s in squares[1:]:
        total = total + s[...]
    return lax.rsqrt(total / D + EPSILON)


def attend_body(members, scale, idx, lens, q0, k0, v, *refs):
    squares, (cosine, sine, gq, gk, wo) = refs[:members], refs[members : members + 5]
    refs = refs[members + 5 :]
    outs, (qr, kr, mixed, lse) = refs[:members], refs[members:]
    me = idx[0]
    total, own = q0.shape
    inv = inverse_rms(squares)
    for n in range(0, total, 128):
        rows = slice(n, n + 128)
        cos, sin = cosine[rows, :], sine[rows, :]
        for i, (raw, gain, out) in enumerate(((q0, gq, qr), (k0, gk, kr))):
            col = to_column(inv[i : i + 1, n : n + 128])
            for h in range(0, own, HD):
                x = raw[rows, h : h + HD] * col * gain[:, h : h + HD].astype(F32)
                out[rows, h : h + HD] = (x * cos + pltpu.roll(x, HD // 2, 1) * sin).astype(BF16)
    step = 256
    for n in range(0, total, step):
        rows = slice(n, n + step)
        at_row, start = doc_start(lens, n, step)
        at_key = iota((step, n + step), 1)
        allowed = (at_key <= at_row) & (at_key >= start)
        for h in range(0, own, HD):
            cols = slice(h, h + HD)
            s = dot_nt(qr[rows, cols], kr[0 : n + step, cols]) * scale
            s = jnp.where(allowed, s, NEG_FILL)
            top = jnp.max(s, axis=-1, keepdims=True)
            p = jnp.exp(s - top)
            norm = jnp.sum(p, axis=-1, keepdims=True)
            lse[rows, h // HD : h // HD + 1] = top + jnp.log(norm)
            p = (p * (1.0 / norm)).astype(BF16)
            mixed[rows, cols] = dot(p, v[0 : n + step, cols]).astype(BF16)
    length = outs[0].shape[0]
    for k in list(range(1, members)) + [0]:
        rows = pl.ds(pl.multiple_of((me ^ k) * length, length), length)
        outs[k][...] = dot(mixed[rows, :], wo[...]).astype(outs[k].dtype)


def place_pieces(members, row, idx, pieces, out):
    me = idx[0]
    own = pieces[0].shape[1]
    for k in range(members):
        cols = pl.ds(pl.multiple_of((me ^ k) * own, own), own)
        out[:, cols] = pieces[k][row, :].astype(out.dtype)


def route_body(members, experts, idx, hidden, own, *refs):
    got, sms = refs[: members - 1], refs[members - 1 : 2 * members - 1]
    h1, packed, route, router, gain = refs[2 * members - 1 :]
    place_pieces(members, slice(0, experts), idx, sms, router)
    place_pieces(members, slice(experts + 1, experts + 2), idx, sms, gain)
    length = hidden.shape[0]
    h = hidden[...].astype(F32) + own[...]
    for g in got:
        h = h + g[...].astype(F32)
    h1[...] = h
    inv = lax.rsqrt(jnp.mean(h * h, axis=-1, keepdims=True) + EPSILON)
    packed[0:length, :] = (h * inv * gain[...]).astype(BF16)
    logits = dot_nt(router[...], packed[0:length, :])
    e = jnp.exp(logits - jnp.max(logits, axis=0, keepdims=True))
    r = e / jnp.sum(e, axis=0, keepdims=True)
    route[...] = r
    packed[length:, :] = jnp.zeros((experts, packed.shape[1]), BF16)
    for i, value in enumerate(split3(r)):
        packed[length:, i * PART : i * PART + length] = value.astype(BF16)


def token_body(members, planes, experts, idx, own, lines, *refs):
    got, (route, h1, packed, grad_out) = refs[: planes - 1], refs[planes - 1 : planes + 3]
    sms = refs[planes + 3 : planes + 3 + members]
    grad, low, small, router, gain = refs[planes + 3 + members :]
    place_pieces(members, slice(0, experts), idx, sms, router)
    place_pieces(members, slice(experts + 1, experts + 2), idx, sms, gain)
    mz = idx[1]
    length = h1.shape[0]
    total = own[...]
    spread = iota((experts, length), 0)
    grad_route = jnp.zeros((experts, length), F32)
    for j in range(planes):
        if j == 0:
            part = lines[...]
        else:
            total = total + got[j - 1][0:length, :].astype(F32)
            part = sum(
                got[j - 1][length : length + 16, i * PART : i * PART + length].astype(F32) for i in range(3)
            )
        z = lax.rem(mz - j + planes, planes)
        for s in range(members):
            grad_route = grad_route + jnp.where(spread == z * members + s, part[s : s + 1], 0.0)
    r = route[...]
    dl = (r * (grad_route - jnp.sum(r * grad_route, axis=0, keepdims=True))).astype(BF16)
    total = total + dot_tn(dl, router[...])
    small[0:experts, :] = dot(dl, packed[0:length, :])
    h = h1[...]
    inv = lax.rsqrt(jnp.mean(h * h, axis=-1, keepdims=True) + EPSILON)
    unit = h * inv
    small[experts : experts + 8, :] = jnp.broadcast_to(
        jnp.sum(total * unit, axis=0, keepdims=True), (8, h.shape[1])
    )
    scaled = total * gain[...]
    back = (scaled - unit * jnp.mean(scaled * unit, axis=-1, keepdims=True)) * inv
    result = grad_out[...].astype(F32) + back
    grad[...] = result
    low[...] = result.astype(BF16)


def attend_back_body(members, scale, idx, lens, *refs):
    ds, squares = refs[:members], refs[members : 2 * members]
    wo, qr, kr, v, lse, q0, k0, cosine, sine, gq, gk = refs[2 * members : 2 * members + 11]
    grads, dv, sq, sk, dots, gains, do, dkt, dvt, sems = refs[2 * members + 11 :]
    me = idx[0]
    length = ds[0].shape[0]
    total, own = q0.shape
    pairs = []
    for k in range(members):
        rows = pl.ds(pl.multiple_of((me ^ k) * length, length), length)
        pairs.append((ds[k], grads.at[rows]))
    copy_all(pairs, sems)
    step = 256
    for n in range(0, total, step):
        do[n : n + step, :] = dot_nt(grads[n : n + step, :], wo[...]).astype(BF16)
    inv = inverse_rms(squares)
    dot_q, dot_k = [0.0] * (total // 128), [0.0] * (total // 128)
    gain_lines = []
    for h in range(0, own, HD):
        cols = slice(h, h + HD)
        for n in range(0, total, step):
            rows = slice(n, n + step)
            keys = slice(0, n + step)
            at_row, start = doc_start(lens, n, step)
            at_key = iota((step, n + step), 1)
            allowed = (at_key <= at_row) & (at_key >= start)
            s = dot_nt(qr[rows, cols], kr[keys, cols]) * scale
            p = jnp.exp(jnp.where(allowed, s - lse[rows, h // HD : h // HD + 1], NEG_FILL))
            dp = dot_nt(do[rows, cols], v[keys, cols])
            delta = jnp.sum(p * dp, axis=-1, keepdims=True)
            grad_s = (p * (dp - delta)).astype(BF16)
            part_v = dot_tn(p.astype(BF16), do[rows, cols])
            part_k = dot_tn(grad_s, qr[rows, cols])
            if n == 0:
                dkt[...] = jnp.zeros(dkt.shape, F32)
                dvt[...] = jnp.zeros(dvt.shape, F32)
            dvt[keys, :] = dvt[keys, :] + part_v
            dkt[keys, :] = dkt[keys, :] + part_k
            sq[rows, cols] = dot(grad_s, kr[keys, cols]) * scale
        dv[:, cols] = dvt[...].astype(BF16)
        gq_sum, gk_sum = jnp.zeros((1, HD), F32), jnp.zeros((1, HD), F32)
        for c in range(total // 128):
            rows = slice(c * 128, c * 128 + 128)
            cos, sin = cosine[rows, :], sine[rows, :]
            for i, raw in enumerate((q0, k0)):
                g = sq[rows, cols] if i == 0 else dkt[rows, :] * scale
                g = g * cos - pltpu.roll(g, HD // 2, 1) * sin
                unit = raw[rows, cols] * to_column(inv[i : i + 1, c * 128 : c * 128 + 128])
                line = jnp.sum(g * unit, axis=0, keepdims=True)
                scaled = g * (gq if i == 0 else gk)[:, cols].astype(F32)
                value = jnp.sum(scaled * unit, axis=1, keepdims=True)
                if i == 0:
                    gq_sum = gq_sum + line
                    sq[rows, cols] = scaled
                    dot_q[c] = dot_q[c] + value
                else:
                    gk_sum = gk_sum + line
                    sk[rows, cols] = scaled
                    dot_k[c] = dot_k[c] + value
        gain_lines.append(jnp.concatenate([gq_sum, gk_sum, jnp.zeros((6, HD), F32)], axis=0))
    gains[...] = jnp.concatenate(gain_lines, axis=1)
    lines = [to_row(jnp.concatenate(x, axis=0)) for x in (dot_q, dot_k)]
    dots[...] = jnp.concatenate(lines + [jnp.zeros((6, total), F32)], axis=0)


def project_back_body(members, planes, idx, sq, sk, dv, q0, k0, a, *refs):
    squares, dots = refs[:members], refs[members : 2 * members]
    d3, keep, away = refs[2 * members :]
    md = idx[2]
    total, own = q0.shape
    inv = inverse_rms(squares)
    mean = dots[0][...]
    for d in dots[1:]:
        mean = mean + d[...]
    mean = mean / D
    for c in range(0, total, 128):
        rows = slice(c, c + 128)
        for i, (scaled, raw) in enumerate(((sq, q0), (sk, k0))):
            col = to_column(inv[i : i + 1, c : c + 128])
            avg = to_column(mean[i : i + 1, c : c + 128])
            unit = raw[rows, :] * col
            d3[rows, i * own : (i + 1) * own] = ((scaled[rows, :] - unit * avg) * col).astype(BF16)
    d3[:, 2 * own :] = dv[...]
    half = own // 2
    for out, side in ((away, 1 - md), (keep, md)):
        for s in range(members):
            cols = pl.ds(pl.multiple_of(s * own + side * half, half), half)
            out[s * half : (s + 1) * half, :] = dot_tn(a[:, cols], d3[...]).astype(out.dtype)


def input_back_body(members, idx, d3, w, *outs):
    me = idx[0]
    length = outs[0].shape[0]
    for k in list(range(1, members)) + [0]:
        rows = pl.ds(pl.multiple_of((me ^ k) * length, length), length)
        outs[k][...] = dot_nt(d3[rows, :], w[...]).astype(outs[k].dtype)


def input_body(members, experts, idx, own, *refs):
    got, sms = refs[: members - 1], refs[members - 1 : 2 * members - 1]
    hidden, grad, out, line, gain = refs[2 * members - 1 :]
    place_pieces(members, slice(experts, experts + 1), idx, sms, gain)
    total = own[...]
    for g in got:
        total = total + g[...].astype(F32)
    h = hidden[...].astype(F32)
    inv = lax.rsqrt(jnp.mean(h * h, axis=-1, keepdims=True) + EPSILON)
    unit = h * inv
    line[...] = jnp.broadcast_to(jnp.sum(total * unit, axis=0, keepdims=True), line.shape)
    scaled = total * gain[...]
    out[...] = grad[...] + (scaled - unit * jnp.mean(scaled * unit, axis=-1, keepdims=True)) * inv


def output_grad_body(idx, mixed, grads, keep, away):
    md = idx[2]
    half = keep.shape[0]
    for out, side in ((away, 1 - md), (keep, md)):
        cols = pl.ds(pl.multiple_of(side * half, half), half)
        out[...] = dot_tn(mixed[:, cols], grads[...]).astype(out.dtype)


def split_body(planes, parts, idx, keep, peer, *outs):
    mz = idx[1]
    slab = keep.shape[0] // (parts * planes)
    for j in range(planes):
        z = lax.rem(mz + j, planes)
        for p in range(parts):
            rows = pl.ds(pl.multiple_of((p * planes + z) * slab, slab), slab)
            value = keep[rows, :] + peer[rows, :].astype(F32)
            outs[j][p * slab : (p + 1) * slab, :] = value.astype(outs[j].dtype)


def add_body(members, idx, *refs):
    values, outs = refs[: len(refs) - members], refs[len(refs) - members :]
    me = idx[0]
    slab = outs[0].shape[0]
    for k in range(members):
        rows = pl.ds(pl.multiple_of((me ^ k) * slab, slab), slab) if members > 1 else slice(0, slab)
        total = values[0][rows, :]
        for value in values[1:]:
            total = total + value[rows, :].astype(F32)
        outs[k][...] = total.astype(BF16)


def merge_body(members, idx, *refs):
    pieces, out = refs[:members], refs[members]
    me = idx[0]
    own = pieces[0].shape[1] // 3
    for k in range(members):
        for i in range(3):
            cols = pl.ds(pl.multiple_of(i * members * own + (me ^ k) * own, own), own)
            out[:, cols] = pieces[k][:, i * own : (i + 1) * own]


def spread_body(planes, idx, *refs):
    pieces, outs = refs[: 2 * planes], refs[2 * planes :]
    mz, md = idx[1], idx[2]
    slab = pieces[0].shape[0]
    width = outs[0].shape[1]
    for c in range(2):
        side = md if c == 0 else 1 - md
        for j in range(planes):
            row = side * (planes * slab) + lax.rem(mz + j, planes) * slab
            rows = pl.ds(pl.multiple_of(row, slab), slab)
            for i, out in enumerate(outs):
                out[rows, :] = pieces[c * planes + j][:, i * width : (i + 1) * width].astype(F32)


def shards(
    hidden_in,
    grad_out,
    doc_lengths,
    expert_ids,
    attn_gain,
    query_gain,
    key_gain,
    mlp_gain,
    w_query,
    w_key,
    w_value,
    w_output,
    w_router,
    w_gate,
    w_up,
    w_down,
):
    length = hidden_in.shape[0]
    members = lax.axis_size("shard")
    planes = lax.axis_size("expert")
    me = lax.axis_index("shard")
    mz = lax.axis_index("expert")
    md = lax.axis_index("dp")
    total = length * members
    experts = planes * members
    capacity = 5 * length * TOP // (4 * experts)
    own = D // members
    local_heads = HEADS // members
    scale = HD ** (-0.5)
    others = range(1, members)

    def swap(value, k):
        return lax.ppermute(value, "shard", [(i, i ^ k) for i in range(members)])

    def fetch_z(value, j):
        return lax.ppermute(value, "expert", [(i, (i - j) % planes) for i in range(planes)])

    def return_z(value, j):
        return lax.ppermute(value, "expert", [(i, (i + j) % planes) for i in range(planes)])

    def swap_dp(value):
        return lax.ppermute(value, "dp", [(0, 1), (1, 0)])

    def exchange(pieces):
        return [pieces[0]] + [swap(pieces[k], k) for k in others]

    def gather_plane(value):
        return exchange([value] * members)

    def gather_z(value):
        return [value] + [fetch_z(value, j) for j in range(1, planes)]

    idx = jnp.stack([me, mz, md]).astype(jnp.int32)
    half = own // 2
    slab = half // planes
    inner = w_gate.shape[2]
    slots = (capacity + 3 + 15) // 16 * 16
    rows = members * slots
    whole = planes * rows
    sms_rows = (experts + 2 + 15) // 16 * 16

    hidden_pieces = gather_plane(hidden_in)
    small = jnp.concatenate([w_router.T, attn_gain[None], mlp_gain[None]], axis=0)
    small = gather_plane(jnp.pad(small, ((0, sms_rows - experts - 2), (0, 0))))
    sent = call(
        functools.partial(prepare_body, members),
        (idx, w_query, w_key, w_value),
        "svvv",
        [((half, 3 * own), BF16)] * (members - 1),
        moved=9 * own * D,
    )
    got = [swap(sent[k - 1], k) for k in others]
    peers = [swap_dp(g) for g in got]

    doc_ids, doc_place = doc_layout(doc_lengths[0], total)
    cosine, sine = rope_tables(doc_place)
    sine = jnp.concatenate([-sine[:, : HD // 2], sine[:, HD // 2 :]], axis=1)
    gain_query, gain_key = query_gain[None], key_gain[None]

    hit = jnp.any(expert_ids[:, :, None] == jnp.arange(experts, dtype=jnp.int32), axis=1)
    before = jnp.triu(jnp.ones((length, length), BF16))
    rank = dot(hit.T.astype(BF16), before).astype(jnp.int32) - 1
    place_z = gather_z(jnp.where(hit.T, rank, -1))
    grads_z = gather_z(grad_out)

    gate_mine, up_mine, down_mine = w_gate[0], w_up[0], w_down[0]
    gate_peer, up_peer, down_peer = swap_dp(gate_mine), swap_dp(up_mine), swap_dp(down_mine)

    query_raw, key_raw, value_rows, attn_input, w_qkv, squares = call(
        functools.partial(project_body, members, experts),
        (idx, *hidden_pieces, *small, w_query, w_key, w_value, *got, *peers),
        "s" + "v" * (2 * members) + "a" * (1 + 2 * members),
        [
            ((total, own), F32),
            ((total, own), F32),
            ((total, own), BF16),
            ((total, D), BF16),
            ((D, 3 * own), BF16),
            ((8, total), F32),
        ],
        scratch=[pltpu.VMEM((1, D), F32), pltpu.SemaphoreType.DMA((1 + 2 * members,))],
        flops=6 * total * D * own,
    )
    squares = gather_plane(squares)
    result = call(
        functools.partial(attend_body, members, scale),
        (idx, doc_lengths, query_raw, key_raw, value_rows, *squares, cosine, sine, gain_query, gain_key, w_output),
        "ss" + "v" * (8 + members),
        [((length, D), F32)]
        + [((length, D), BF16)] * (members - 1)
        + [((total, own), BF16)] * 3
        + [((total, 128), F32)],
        flops=8 * total * total * own + 2 * total * own * D,
    )
    partial = exchange(result[:members])
    query_heads, key_heads, mixed, log_total = result[members:]
    residual, packed, route = call(
        functools.partial(route_body, members, experts),
        (idx, hidden_in, *partial, *small),
        "s" + "v" * (1 + 2 * members),
        [((length, D), F32), ((length + experts, D), BF16), ((experts, length), F32)],
        scratch=[pltpu.VMEM((experts, D), BF16), pltpu.VMEM((1, D), F32)],
    )

    def dispatch(source, j, gated, after=()):
        return call(
            functools.partial(dispatch_body, gated, members, capacity, slots),
            (idx, place_z[j], source),
            "svv",
            [((slots, D), BF16)] * members,
            flops=2 * members * slots * length * D,
            after=after,
        )

    input_z = gather_z(packed)
    grad_pieces, slot_pieces, blocks_gm, blocks_dz, blocks_du, back = [], [], [], [], [], []
    weights = (gate_mine, gate_peer, up_mine, up_peer, down_mine, down_peer)
    order = [squares[1:], [residual]]
    for j in range(planes):
        pieces = exchange(dispatch(input_z[j], j, True))
        slot_pieces += pieces
        after = order[j] if j < 2 else back[j - 2][1:2]
        grads = exchange(dispatch(grads_z[j], j, False, after))
        grad_pieces += grads
        result = call(
            functools.partial(expert_body, members, capacity, slots, 0),
            (idx, *pieces, *grads, *weights),
            "s" + "a" * (2 * members) + "v" * 6,
            [((slots, D), BF16)] * members + [((rows, inner), BF16)] * 3,
            scratch=[
                pltpu.VMEM((rows, D), BF16),
                pltpu.VMEM((rows, D), BF16),
                pltpu.SemaphoreType.DMA((2 * members,)),
            ],
            vmem=48,
            flops=10 * rows * D * inner,
        )
        back.append(exchange(result[:members]))
        blocks_gm.append(result[members])
        blocks_dz.append(result[members + 1])
        blocks_du.append(result[members + 2])

    def collect(pieces, j, graded):
        extra_rows = 16 if graded and j > 0 else 0
        outs = [((length + extra_rows, D), F32 if j == 0 else BF16)]
        if graded and j == 0:
            outs.append(((16, length), F32))
        return call(
            functools.partial(collect_body, graded, j > 0, members, capacity, slots),
            (idx, place_z[j], *pieces),
            "sv" + "a" * members,
            outs,
            scratch=[
                pltpu.VMEM((rows, D), BF16),
                pltpu.VMEM((rows, length), BF16),
                pltpu.SemaphoreType.DMA((members,)),
            ],
            flops=2 * rows * length * D,
        )

    sums = [collect(back[j], j, True) for j in range(planes)]
    returned = [return_z(sums[j][0], j) for j in range(1, planes)]
    grad_residual, grad_low, small_part = call(
        functools.partial(token_body, members, planes, experts),
        (idx, *sums[0], *returned, route, residual, packed, grad_out, *small),
        "s" + "v" * (2 + planes - 1 + 4 + members),
        [((length, D), F32), ((length, D), BF16), ((experts + 8, D), F32)],
        scratch=[pltpu.VMEM((experts, D), BF16), pltpu.VMEM((1, D), F32)],
    )
    grad_all = gather_plane(grad_low)

    expert_sum = residual
    for first, last, after in ((0, planes // 2, [s[0] for s in sums[1:]]), (planes // 2, planes, grad_all[1:])):
        span = last - first
        weighted = call(
            functools.partial(down_body, span, members, slots),
            (idx, *blocks_gm[first:last], down_mine, down_peer),
            "s" + "v" * (span + 2),
            [((span * slots, D), BF16)] * members,
            flops=2 * span * rows * D * inner,
            after=after,
        )
        weighted = exchange(weighted)
        for j in range(first, last):
            at_row = (j - first) * slots
            part = collect([w[at_row : at_row + slots] for w in weighted], j, False)[0]
            if j > 0:
                part = return_z(part, j).astype(F32)
            expert_sum = expert_sum + part
    block_out = expert_sum.astype(BF16)

    half_d = D // 2

    def row_grad(blocks):
        return call(
            functools.partial(row_grad_body, (len(slot_pieces), planes), slots),
            (idx, *slot_pieces, *blocks),
            "s" + "a" * (len(slot_pieces) + planes),
            [((half_d, inner), F32), ((half_d, inner), BF16)],
            scratch=[
                pltpu.VMEM((whole, D), BF16),
                pltpu.VMEM((whole, inner), BF16),
                pltpu.SemaphoreType.DMA((len(slot_pieces) + planes,)),
            ],
            vmem=48,
            flops=2 * whole * D * inner,
        )

    grad_gate, away = row_grad(blocks_dz)
    grad_gate = (grad_gate + swap_dp(away).astype(F32))[None]
    grad_up, away = row_grad(blocks_du)
    grad_up = (grad_up + swap_dp(away).astype(F32))[None]
    grad_down, away = call(
        functools.partial(col_grad_body, planes, members, slots),
        (idx, *blocks_gm, *grad_pieces),
        "s" + "a" * (planes + len(grad_pieces)),
        [((inner, half_d), F32), ((inner, half_d), BF16)],
        scratch=[
            pltpu.VMEM((whole, inner), BF16),
            pltpu.VMEM((whole, D), BF16),
            pltpu.SemaphoreType.DMA((planes + planes * members,)),
        ],
        vmem=48,
        flops=2 * whole * D * inner,
    )
    grad_down = (grad_down + swap_dp(away).astype(F32))[None]

    grads, grad_value, scaled_query, scaled_key, dots, grad_gains = call(
        functools.partial(attend_back_body, members, scale),
        (
            idx,
            doc_lengths,
            *grad_all,
            *squares,
            w_output,
            query_heads,
            key_heads,
            value_rows,
            log_total,
            query_raw,
            key_raw,
            cosine,
            sine,
            gain_query,
            gain_key,
        ),
        "ss" + "a" * members + "v" * (members + 11),
        [
            ((total, D), BF16),
            ((total, own), BF16),
            ((total, own), F32),
            ((total, own), F32),
            ((8, total), F32),
            ((8, own), F32),
        ],
        scratch=[
            pltpu.VMEM((total, own), BF16),
            pltpu.VMEM((total, HD), F32),
            pltpu.VMEM((total, HD), F32),
            pltpu.SemaphoreType.DMA((members,)),
        ],
        flops=20 * total * total * own // 2,
    )
    dots = gather_plane(dots)
    grad_raw, keep, away = call(
        functools.partial(project_back_body, members, planes),
        (idx, scaled_query, scaled_key, grad_value, query_raw, key_raw, attn_input, *squares, *dots),
        "s" + "v" * (6 + 2 * members),
        [((total, 3 * own), BF16), ((D // 2, 3 * own), F32), ((D // 2, 3 * own), BF16)],
        vmem=48,
        flops=6 * total * D * own,
    )

    def scatter_z(keep, away, parts, holders):
        height, width = keep.shape
        pieces = call(
            functools.partial(split_body, planes, parts),
            (idx, keep, swap_dp(away)),
            "svv",
            [((height // planes, width), F32)] + [((height // planes, width), BF16)] * (planes - 1),
        )
        pieces = [pieces[0]] + [return_z(pieces[j], j) for j in range(1, planes)]
        return call(
            functools.partial(add_body, holders),
            (idx, *pieces),
            "s" + "v" * planes,
            [((height // planes // holders, width), BF16)] * holders,
        )

    def spread_z(piece, count):
        pieces = gather_z(piece)
        pieces = pieces + [swap_dp(p) for p in pieces]
        return call(
            functools.partial(spread_body, planes),
            (idx, *pieces),
            "s" + "v" * (2 * planes),
            [((own, D), F32)] * count,
        )

    summed = exchange(scatter_z(keep, away, members, members))
    piece = call(
        functools.partial(merge_body, members),
        (idx, *summed),
        "s" + "v" * members,
        [((slab, 3 * D), BF16)],
    )[0]
    grad_query, grad_key, grad_value_w = spread_z(piece, 3)

    keep, away = call(
        output_grad_body,
        (idx, mixed, grads),
        "svv",
        [((half, D), F32), ((half, D), BF16)],
        flops=2 * total * own * D,
    )
    grad_output = spread_z(scatter_z(keep, away, 1, 1)[0], 1)[0]

    partial = call(
        functools.partial(input_back_body, members),
        (idx, grad_raw, w_qkv),
        "svv",
        [((length, D), F32)] + [((length, D), BF16)] * (members - 1),
        flops=6 * total * D * own,
    )
    partial = exchange(partial)
    grad_in, line = call(
        functools.partial(input_body, members, experts),
        (idx, *partial, *small, hidden_in, grad_residual),
        "s" + "v" * (2 * members + 2),
        [((length, D), F32), ((8, D), F32)],
        scratch=[pltpu.VMEM((1, D), F32)],
    )

    small_part = jnp.concatenate([small_part[: experts + 1], line[:1]], axis=0)
    small_pieces = small_part.reshape(experts + 2, members, own).transpose(1, 0, 2)
    small_sum = at(small_pieces, me)
    for k in others:
        small_sum = small_sum + swap(at(small_pieces, me ^ k), k)
    small_sum = jnp.concatenate([small_sum, grad_gains[:2]], axis=0)
    small_sum = small_sum + swap_dp(small_sum)
    stack = jnp.stack(gather_z(small_sum))
    small_total = at(stack, (0 - mz) % planes)
    for z in range(1, planes):
        small_total = small_total + at(stack, (z - mz) % planes)
    return (
        block_out,
        grad_in,
        small_total[experts + 1],
        small_total[experts + 2],
        small_total[experts + 3],
        small_total[experts],
        grad_query,
        grad_key,
        grad_value_w,
        grad_output,
        small_total[:experts].T,
        grad_gate,
        grad_up,
        grad_down,
    )


def solution(mesh):
    return jax.shard_map(
        shards,
        mesh=mesh,
        in_specs=(
            P(("dp", "expert", "shard"), None),
            P(("dp", "expert", "shard"), None),
            P(("dp", "expert"), None),
            P(("dp", "expert", "shard"), None),
            P("shard"),
            P("shard"),
            P("shard"),
            P("shard"),
            P("shard", None),
            P("shard", None),
            P("shard", None),
            P("shard", None),
            P("shard", None),
            P(("expert", "shard"), "dp", None),
            P(("expert", "shard"), "dp", None),
            P(("expert", "shard"), None, "dp"),
        ),
        out_specs=(
            P(("dp", "expert", "shard"), None),
            P(("dp", "expert", "shard"), None),
            P("shard"),
            P("shard"),
            P("shard"),
            P("shard"),
            P("shard", None),
            P("shard", None),
            P("shard", None),
            P("shard", None),
            P("shard", None),
            P(("expert", "shard"), "dp", None),
            P(("expert", "shard"), "dp", None),
            P(("expert", "shard"), None, "dp"),
        ),
        check_vma=False,
    )
```

```python
import functools
import math

import jax
import jax.numpy as jnp
from jax import lax
from jax.experimental import pallas as pl
from jax.experimental.pallas import tpu as pltpu
from jax.sharding import PartitionSpec as P

D = 2048
HEADS = 16
HD = 128
TOP = 8
DOCS = 4

EPSILON = 1e-05
ROPE_BASE = 10000.0
NEG_FILL = -1e30

F32 = jnp.float32
BF16 = jnp.bfloat16


def dot(a, b):
    return jnp.dot(a, b, preferred_element_type=F32)


def dot_nt(a, b):
    return lax.dot_general(a, b, (((1,), (1,)), ((), ())), preferred_element_type=F32)


def dot_tn(a, b):
    return lax.dot_general(a, b, (((0,), (0,)), ((), ())), preferred_element_type=F32)


def at(stack, index):
    return lax.dynamic_index_in_dim(stack, index, 0, keepdims=False)


def doc_layout(lengths, total):
    doc_ends = jnp.cumsum(lengths)
    doc_starts = doc_ends - lengths
    places = jnp.arange(total, dtype=jnp.int32)
    doc_ids = jnp.sum((places[:, None] >= doc_ends[None, :]).astype(jnp.int32), axis=1)
    owner = doc_ids[:, None] == jnp.arange(DOCS, dtype=jnp.int32)[None, :]
    begins = jnp.sum(jnp.where(owner, doc_starts[None, :], 0), axis=1)
    return doc_ids, places - begins


def rope_tables(doc_place):
    half_size = HD // 2
    freqs = jnp.exp(-math.log(ROPE_BASE) * 2.0 * jnp.arange(half_size, dtype=F32) / HD)
    angles = doc_place.astype(F32)[:, None] * freqs
    angles = jnp.concatenate([angles, angles], axis=-1)
    return jnp.cos(angles), jnp.sin(angles)


PART = 256
MIB = 1024 * 1024


def call(body, args, kinds, outs, scratch=(), vmem=40, after=()):
    spaces = {"v": pltpu.VMEM, "s": pltpu.SMEM, "a": pl.ANY, "d": pl.ANY}
    count, moved = len(args), [i for i, kind in enumerate(kinds) if kind == "d"]
    extra = [pltpu.VMEM(args[i].shape, args[i].dtype) for i in moved]
    if moved:
        extra.append(pltpu.SemaphoreType.DMA((len(moved),)))

    def run(*refs):
        given, rest = list(refs[:count]), list(refs[count + len(after) :])
        if moved:
            held, sems = rest[-len(moved) - 1 : -1], rest[-1]
            rest = rest[: -len(moved) - 1]
            copy_all([(given[i], to) for i, to in zip(moved, held)], sems)
            for i, to in zip(moved, held):
                given[i] = to
        body(*given, *rest)

    return pl.pallas_call(
        run,
        out_shape=[jax.ShapeDtypeStruct(shape, dtype) for shape, dtype in outs],
        in_specs=[pl.BlockSpec(memory_space=spaces[kind]) for kind in kinds + "a" * len(after)],
        out_specs=[pl.BlockSpec(memory_space=pltpu.VMEM) for _ in outs],
        scratch_shapes=[*scratch, *extra],
        compiler_params=pltpu.CompilerParams(vmem_limit_bytes=vmem * MIB),
        cost_estimate=pl.CostEstimate(flops=1000, bytes_accessed=1000, transcendentals=0),
    )(*args, *after)


def copy_all(pairs, sems):
    copies = [pltpu.make_async_copy(a, b, sems.at[i]) for i, (a, b) in enumerate(pairs)]
    for c in copies:
        c.start()
    for c in copies:
        c.wait()


def iota(shape, axis):
    return lax.broadcasted_iota(jnp.int32, shape, axis)


def split3(x):
    hi = x.astype(BF16).astype(F32)
    mid = (x - hi).astype(BF16).astype(F32)
    lo = (x - hi - mid).astype(BF16).astype(F32)
    return hi, mid, lo


def pick_rows(place, slots):
    slot = iota((slots, place.shape[1]), 0).astype(F32)
    return jnp.where(slot == place, 1.0, 0.0).astype(BF16)


def dispatch_body(shifts, gated, members, planes, capacity, slots, idx, places, source, *refs):
    outs, (rows, sems) = refs[:members], refs[members:]
    experts, length = places.shape[1:]
    me, mz = idx[0], idx[1]
    copies = []
    for n, shift in enumerate(shifts):
        z = lax.rem(mz + shift, planes)
        block = source.at[z] if len(source.shape) == 3 else source
        copies.append(pltpu.make_async_copy(block, rows.at[n], sems.at[n]))
    for copy in copies:
        copy.start()
    for n, shift in enumerate(shifts):
        z = lax.rem(mz + shift, planes)
        span = slice(n * slots, (n + 1) * slots)
        copies[n].wait()
        for k in range(members):
            expert = mz * members + (me ^ k)
            pick = pick_rows(places[z, pl.ds(expert, 1), :], slots)
            result = dot(pick, rows[n, 0:length, :])
            outs[k][span, :] = result.astype(BF16)
            if gated:
                head = result[:, 0:128]
                row = iota((slots, 128), 0)
                for part in range(3):
                    table = rows[n, length : length + experts, part * PART : part * PART + length].astype(F32)
                    gate = jnp.sum(jnp.where(iota(table.shape, 0) == expert, table, 0.0), axis=0, keepdims=True)
                    gate = jnp.broadcast_to(gate, (8, length)).astype(BF16)
                    slot = dot_nt(gate, pick)[0:1, :]
                    if slots < 128:
                        slot = jnp.concatenate([slot, jnp.zeros((1, 128 - slots), F32)], axis=1)
                    head = head + jnp.where(row == capacity + part, slot, 0.0)
                outs[k][span, 0:128] = head.astype(BF16)


def expert_body(where, members, capacity, slots, idx, *refs):
    groups = 1 + max(g for g, _ in where)
    xs, cs = refs[:members], refs[members : members + groups * members]
    refs = refs[members + groups * members :]
    weights, rest = refs[:6], refs[6:]
    ds, (gm, dz, du) = rest[:members], rest[members : members + 3]
    x, c, wg, wu, wd, sems = rest[members + 3 :]
    md = idx[2]
    half = wd.shape[2]
    pairs = []
    pieces = [(i, k) for i in range(len(where)) for k in range(members)]
    for n, (i, k) in enumerate(pieces):
        g, first = where[i]
        to = pl.ds(n * slots, slots)
        pairs.append((xs[k].at[pl.ds(i * slots, slots)], x.at[to]))
        pairs.append((cs[g * members + k].at[pl.ds(first, slots)], c.at[to]))
    for n, side in ((0, md), (1, 1 - md)):
        rows = pl.ds(pl.multiple_of(side * half, half), half)
        pairs += [(weights[n], wg.at[rows]), (weights[2 + n], wu.at[rows])]
        pairs.append((weights[4 + n], wd.at[side]))
    copy_all(pairs, sems)
    inner = wg.shape[1]
    rows = len(pieces) * slots
    eye = iota((slots, 128), 0) == iota((slots, 128), 1)
    row = iota((slots, 128), 0)
    gates = []
    for n in range(len(pieces)):
        part = x[n * slots : (n + 1) * slots, 0:128].astype(F32)
        line = jnp.sum(
            jnp.where((row >= capacity) & (row < capacity + 3), part, 0.0), axis=0, keepdims=True
        )
        gates.append(jnp.sum(jnp.where(eye, line, 0.0), axis=1, keepdims=True))
    gate = jnp.concatenate(gates, axis=0)
    gate_grad = jnp.zeros((rows, 1), F32)
    step = 256 if rows <= 1024 else 128
    for n in range(0, inner, step):
        cols = slice(n, n + step)
        z = dot(x[...], wg[:, cols])
        u = dot(x[...], wu[:, cols])
        raw = dot_nt(c[:, 0:half], wd[0, cols, :]) + dot_nt(c[:, half:], wd[1, cols, :])
        sig = 1.0 / (1.0 + jnp.exp(-z))
        silu = z * sig
        middle = silu * u
        gate_grad = gate_grad + jnp.sum(
            raw * middle.astype(BF16).astype(F32), axis=1, keepdims=True
        )
        gm[:, cols] = (gate * middle).astype(BF16)
        raw = raw * gate
        dz[:, cols] = (raw * u * sig * (1.0 + z * (1.0 - sig))).astype(BF16)
        du[:, cols] = (raw * silu).astype(BF16)
    for n in range(0, wg.shape[0], 2 * step):
        cols = slice(n, n + 2 * step)
        result = dot_nt(dz[...], wg[cols, :]) + dot_nt(du[...], wu[cols, :])
        for m, (i, k) in enumerate(pieces):
            ds[k][i * slots : (i + 1) * slots, cols] = result[m * slots : (m + 1) * slots].astype(BF16)
    for m, (i, k) in enumerate(pieces):
        span = slice(i * slots, (i + 1) * slots)
        col = gate_grad[m * slots : (m + 1) * slots]
        line = jnp.sum(jnp.where(eye, col, 0.0), axis=0, keepdims=True)
        head = ds[k][span, 0:128].astype(F32)
        for part, value in enumerate(split3(line)):
            head = head + jnp.where(row == capacity + part, value, 0.0)
        ds[k][span, 0:128] = head.astype(BF16)


def collect_body(shift, first, graded, low, members, planes, capacity, slots, idx, places, *refs):
    rows, outs, (stack, pick, sems) = refs[:members], refs[members:-3], refs[-3:]
    length = places.shape[2]
    me, mz = idx[0], idx[1]
    z = lax.rem(mz + shift, planes)
    copies = [
        pltpu.make_async_copy(rows[k].at[pl.ds(first, slots)], stack.at[pl.ds(k * slots, slots)], sems.at[k])
        for k in range(members)
    ]
    for copy in copies:
        copy.start()
    for k in range(members):
        expert = mz * members + (me ^ k)
        pick[k * slots : (k + 1) * slots, :] = pick_rows(places[z, pl.ds(expert, 1), :], slots)
    for copy in copies:
        copy.wait()
    out = outs[0]
    result = dot_tn(pick[...], stack[...])
    out[0:length, :] = result.astype(out.dtype)
    if not graded:
        return
    slab = iota((16, length), 0)
    lines = jnp.zeros((16, length), F32)
    row = iota((slots, 128), 0)
    for k in range(members):
        head = stack[k * slots : (k + 1) * slots, 0:128].astype(F32)
        pieces = [
            jnp.sum(jnp.where(row == capacity + i, head, 0.0), axis=0, keepdims=True) for i in range(3)
        ]
        pieces = jnp.concatenate(pieces + [jnp.zeros((5, 128), F32)], axis=0).astype(BF16)
        line = jnp.sum(
            dot(pieces[:, 0:slots], pick[k * slots : (k + 1) * slots, :]), axis=0, keepdims=True
        )
        lines = lines + jnp.where(slab == (me ^ k), line, 0.0)
    if low:
        out[length : length + 16, :] = jnp.zeros((16, out.shape[1]), BF16)
        for i, value in enumerate(split3(lines)):
            out[length : length + 16, i * PART : i * PART + length] = value.astype(BF16)
    else:
        outs[1][...] = lines


def load_pieces(where, arrays, slots, out):
    return [
        (arrays[g].at[pl.ds(first, slots)], out.at[pl.ds(i * slots, slots)])
        for i, (g, first) in enumerate(where)
    ]


def load_blocks(blocks, out):
    pairs, first = [], 0
    for block in blocks:
        pairs.append((block, out.at[pl.ds(first, block.shape[0])]))
        first += block.shape[0]
    return pairs


def row_grad_body(where, slots, idx, *refs):
    count = 1 + max(g for g, _ in where)
    pieces, blocks = refs[:count], refs[count:-5]
    keep, away, a, b, sems = refs[-5:]
    copy_all(load_pieces(where, pieces, slots, a) + load_blocks(blocks, b), sems)
    md = idx[2]
    step, half = 256, keep.shape[0]
    for out, side in ((away, 1 - md), (keep, md)):
        for n in range(0, half, step):
            cols = pl.ds(pl.multiple_of(side * half + n, step), step)
            out[n : n + step, :] = dot_tn(a[:, cols], b[...]).astype(out.dtype)


def col_grad_body(where, slots, idx, *refs):
    count = 1 + max(g for g, _ in where)
    pieces, blocks = refs[:count], refs[count:-5]
    keep, away, b, a, sems = refs[-5:]
    copy_all(load_pieces(where, pieces, slots, b) + load_blocks(blocks, a), sems)
    md = idx[2]
    step, half = 256, keep.shape[1]
    for n in range(0, keep.shape[0], step):
        lhs = a[:, n : n + step]
        for out, side in ((away, 1 - md), (keep, md)):
            cols = pl.ds(pl.multiple_of(side * half, half), half)
            out[n : n + step, :] = dot_tn(lhs, b[:, cols]).astype(out.dtype)


def down_body(where, members, slots, idx, *refs):
    count = len(refs) - members - 2
    blocks, (mine, peer), outs = refs[:count], refs[count : count + 2], refs[count + 2 :]
    md = idx[2]
    half = mine.shape[1]
    rows = members * slots
    for n, (g, first) in enumerate(where):
        for w, side in ((mine, md), (peer, 1 - md)):
            cols = pl.ds(pl.multiple_of(side * half, half), half)
            result = dot(blocks[g][first : first + rows, :], w[...])
            for k in range(members):
                outs[k][n * slots : (n + 1) * slots, cols] = result[k * slots : (k + 1) * slots].astype(BF16)


def to_row(column):
    eye = iota((128, 128), 0) == iota((128, 128), 1)
    return jnp.concatenate(
        [
            jnp.sum(jnp.where(eye, column[i : i + 128], 0.0), axis=0, keepdims=True)
            for i in range(0, column.shape[0], 128)
        ],
        axis=1,
    )


def to_column(line):
    eye = iota((128, 128), 0) == iota((128, 128), 1)
    return jnp.sum(jnp.where(eye, line, 0.0), axis=1, keepdims=True)


def prepare_body(choice, members, idx, wq, wk, wv, *outs):
    me, md = idx[0], idx[2]
    half = outs[0].shape[0]
    own = wq.shape[1] // members
    rows = pl.ds(pl.multiple_of(md * half, half), half)
    for n, k in enumerate(choice):
        cols = pl.ds(pl.multiple_of((me ^ k) * own, own), own)
        for i, w in enumerate((wq, wk, wv)):
            outs[n][:, i * own : (i + 1) * own] = w[rows, cols]


def project_body(members, experts, idx, *refs):
    hs = refs[:members]
    refs = refs[members:]
    ws, got, peer = refs[:3], refs[3 : 2 + members], refs[2 + members : 1 + 2 * members]
    q0, k0, v, a, w, squares, gain, sems = refs[1 + 2 * members :]
    me, md = idx[0], idx[2]
    total = a.shape[0]
    length = total // members
    own = q0.shape[1]
    half = own // 2
    copies = []
    base = pl.multiple_of(me * own, own)
    for i in range(3):
        copies.append((ws[i].at[:, pl.ds(base, own)], w.at[pl.ds(base, own), i * own : (i + 1) * own]))
    for k in range(1, members):
        for side, source in ((md, got), (1 - md, peer)):
            row = pl.multiple_of((me ^ k) * own + side * half, half)
            copies.append((source[k - 1], w.at[pl.ds(row, half)]))
    copies = [pltpu.make_async_copy(s, d, sems.at[i]) for i, (s, d) in enumerate(copies)]
    for c in copies:
        c.start()
    place_gain(members, experts, length, 0, idx, hs, gain)
    for k in range(members):
        h = hs[k][0:length, :].astype(F32)
        inv = lax.rsqrt(jnp.mean(h * h, axis=-1, keepdims=True) + EPSILON)
        rows = pl.ds(pl.multiple_of((me ^ k) * length, length), length)
        a[rows, :] = (h * inv * gain[...]).astype(BF16)
    for c in copies:
        c.wait()
    step = 256
    sums = [[], []]
    for n in range(0, total, step):
        rows = slice(n, n + step)
        for i, out in enumerate((q0, k0)):
            raw = dot(a[rows, :], w[:, i * own : (i + 1) * own])
            out[rows, :] = raw
            sums[i].append(jnp.sum(raw * raw, axis=1, keepdims=True))
        v[rows, :] = dot(a[rows, :], w[:, 2 * own :]).astype(BF16)
    lines = [to_row(jnp.concatenate(s, axis=0)) for s in sums]
    squares[...] = jnp.concatenate(lines + [jnp.zeros((6, total), F32)], axis=0)


def doc_start(lens, first, count):
    end0 = lens[0, 0]
    end1 = end0 + lens[0, 1]
    end2 = end1 + lens[0, 2]
    at_row = iota((count, 1), 0) + first
    later = jnp.where(at_row < end2, end1, at_row)
    start = jnp.where(at_row < end0, 0, jnp.where(at_row < end1, end0, later))
    return at_row, start


def inverse_rms(squares):
    total = squares[0][...]
    for s in squares[1:]:
        total = total + s[...]
    return lax.rsqrt(total / D + EPSILON)


def attend_body(members, scale, idx, lens, q0, k0, v, *refs):
    squares, (cosine, sine, gq, gk, wo) = refs[:members], refs[members : members + 5]
    refs = refs[members + 5 :]
    outs, (qr, kr, mixed, lse) = refs[:members], refs[members:]
    me = idx[0]
    total, own = q0.shape
    inv = inverse_rms(squares)
    for n in range(0, total, 128):
        rows = slice(n, n + 128)
        cos, sin = cosine[rows, :], sine[rows, :]
        for i, (raw, gain, out) in enumerate(((q0, gq, qr), (k0, gk, kr))):
            col = to_column(inv[i : i + 1, n : n + 128])
            for h in range(0, own, HD):
                x = raw[rows, h : h + HD] * col * gain[:, h : h + HD].astype(F32)
                out[rows, h : h + HD] = (x * cos + pltpu.roll(x, HD // 2, 1) * sin).astype(BF16)
    step = 256
    for n in range(0, total, step):
        rows = slice(n, n + step)
        at_row, start = doc_start(lens, n, step)
        at_key = iota((step, n + step), 1)
        allowed = (at_key <= at_row) & (at_key >= start)
        for h in range(0, own, HD):
            cols = slice(h, h + HD)
            s = dot_nt(qr[rows, cols], kr[0 : n + step, cols]) * scale
            s = jnp.where(allowed, s, NEG_FILL)
            top = jnp.max(s, axis=-1, keepdims=True)
            p = jnp.exp(s - top)
            norm = jnp.sum(p, axis=-1, keepdims=True)
            lse[rows, h // HD : h // HD + 1] = top + jnp.log(norm)
            p = (p * (1.0 / norm)).astype(BF16)
            mixed[rows, cols] = dot(p, v[0 : n + step, cols]).astype(BF16)
    length = outs[0].shape[0]
    for k in list(range(1, members)) + [0]:
        rows = pl.ds(pl.multiple_of((me ^ k) * length, length), length)
        outs[k][...] = dot(mixed[rows, :], wo[...]).astype(outs[k].dtype)


def place_router(members, experts, length, idx, pieces, out):
    me = idx[0]
    own = out.shape[1] // members
    count = experts // members
    for k in range(members):
        cols = pl.ds(pl.multiple_of((me ^ k) * own, own), own)
        for i in range(members):
            part = pieces[k][length:, i * own : (i + 1) * own].astype(F32)
            out[i * count : (i + 1) * count, cols] = part[0:count]


def place_gain(members, experts, length, part, idx, pieces, out):
    me = idx[0]
    own = out.shape[1] // members
    row = experts // members
    for k in range(members):
        cols = pl.ds(pl.multiple_of((me ^ k) * own, own), own)
        value = pieces[k][length:, part * own : (part + 1) * own].astype(F32)
        out[:, cols] = value[row : row + 1]


def route_body(members, experts, idx, hidden, own, *refs):
    got, sms = refs[: members - 1], refs[members - 1 : 2 * members - 1]
    h1, packed, route, router, gain = refs[2 * members - 1 :]
    length = hidden.shape[0]
    place_router(members, experts, length, idx, sms, router)
    place_gain(members, experts, length, 1, idx, sms, gain)
    h = hidden[...].astype(F32) + own[...]
    for g in got:
        h = h + g[...].astype(F32)
    h1[...] = h
    inv = lax.rsqrt(jnp.mean(h * h, axis=-1, keepdims=True) + EPSILON)
    packed[0:length, :] = (h * inv * gain[...]).astype(BF16)
    logits = dot_nt(router[...].astype(BF16), packed[0:length, :])
    e = jnp.exp(logits - jnp.max(logits, axis=0, keepdims=True))
    r = e / jnp.sum(e, axis=0, keepdims=True)
    route[...] = r
    packed[length:, :] = jnp.zeros((experts, packed.shape[1]), BF16)
    for i, value in enumerate(split3(r)):
        packed[length:, i * PART : i * PART + length] = value.astype(BF16)


def token_body(members, planes, experts, idx, own, lines, *refs):
    got, (route, h1, packed, grad_out) = refs[: planes - 1], refs[planes - 1 : planes + 3]
    sms = refs[planes + 3 : planes + 3 + members]
    grad, low, small, router, gain = refs[planes + 3 + members :]
    mz = idx[1]
    length = h1.shape[0]
    place_router(members, experts, length, idx, sms, router)
    place_gain(members, experts, length, 1, idx, sms, gain)
    total = own[...]
    spread = iota((experts, length), 0)
    grad_route = jnp.zeros((experts, length), F32)
    for j in range(planes):
        if j == 0:
            part = lines[...]
        else:
            total = total + got[j - 1][0:length, :].astype(F32)
            part = sum(
                got[j - 1][length : length + 16, i * PART : i * PART + length].astype(F32) for i in range(3)
            )
        z = lax.rem(mz - j + planes, planes)
        for s in range(members):
            grad_route = grad_route + jnp.where(spread == z * members + s, part[s : s + 1], 0.0)
    r = route[...]
    dl = (r * (grad_route - jnp.sum(r * grad_route, axis=0, keepdims=True))).astype(BF16)
    total = total + dot_tn(dl, router[...].astype(BF16))
    small[0:experts, :] = dot(dl, packed[0:length, :])
    h = h1[...]
    inv = lax.rsqrt(jnp.mean(h * h, axis=-1, keepdims=True) + EPSILON)
    unit = h * inv
    small[experts : experts + 8, :] = jnp.broadcast_to(
        jnp.sum(total * unit, axis=0, keepdims=True), (8, h.shape[1])
    )
    scaled = total * gain[...]
    back = (scaled - unit * jnp.mean(scaled * unit, axis=-1, keepdims=True)) * inv
    result = grad_out[...].astype(F32) + back
    grad[...] = result
    low[...] = result.astype(BF16)


def attend_back_body(members, scale, idx, lens, *refs):
    ds, squares = refs[:members], refs[members : 2 * members]
    wo, qr, kr, v, lse, q0, k0, cosine, sine, gq, gk = refs[2 * members : 2 * members + 11]
    dv, sq, sk, dots, gains, grads, do, dkt, dvt, sems = refs[2 * members + 11 :]
    me = idx[0]
    length = ds[0].shape[0]
    total, own = q0.shape
    pairs = []
    for k in range(members):
        rows = pl.ds(pl.multiple_of((me ^ k) * length, length), length)
        pairs.append((ds[k], grads.at[rows]))
    copy_all(pairs, sems)
    step = 256
    for n in range(0, total, step):
        do[n : n + step, :] = dot_nt(grads[n : n + step, :], wo[...]).astype(BF16)
    inv = inverse_rms(squares)
    dot_q, dot_k = [0.0] * (total // 128), [0.0] * (total // 128)
    gain_lines = []
    for h in range(0, own, HD):
        cols = slice(h, h + HD)
        for n in range(0, total, step):
            rows = slice(n, n + step)
            keys = slice(0, n + step)
            at_row, start = doc_start(lens, n, step)
            at_key = iota((step, n + step), 1)
            allowed = (at_key <= at_row) & (at_key >= start)
            s = dot_nt(qr[rows, cols], kr[keys, cols]) * scale
            p = jnp.exp(jnp.where(allowed, s - lse[rows, h // HD : h // HD + 1], NEG_FILL))
            dp = dot_nt(do[rows, cols], v[keys, cols])
            delta = jnp.sum(p * dp, axis=-1, keepdims=True)
            grad_s = (p * (dp - delta)).astype(BF16)
            part_v = dot_tn(p.astype(BF16), do[rows, cols])
            part_k = dot_tn(grad_s, qr[rows, cols])
            if n == 0:
                dkt[...] = jnp.zeros(dkt.shape, F32)
                dvt[...] = jnp.zeros(dvt.shape, F32)
            dvt[keys, :] = dvt[keys, :] + part_v
            dkt[keys, :] = dkt[keys, :] + part_k
            sq[rows, cols] = dot(grad_s, kr[keys, cols]) * scale
        dv[:, cols] = dvt[...].astype(BF16)
        gq_sum, gk_sum = jnp.zeros((1, HD), F32), jnp.zeros((1, HD), F32)
        for c in range(total // 128):
            rows = slice(c * 128, c * 128 + 128)
            cos, sin = cosine[rows, :], sine[rows, :]
            for i, raw in enumerate((q0, k0)):
                g = sq[rows, cols] if i == 0 else dkt[rows, :] * scale
                g = g * cos - pltpu.roll(g, HD // 2, 1) * sin
                unit = raw[rows, cols] * to_column(inv[i : i + 1, c * 128 : c * 128 + 128])
                line = jnp.sum(g * unit, axis=0, keepdims=True)
                scaled = g * (gq if i == 0 else gk)[:, cols].astype(F32)
                value = jnp.sum(scaled * unit, axis=1, keepdims=True)
                if i == 0:
                    gq_sum = gq_sum + line
                    sq[rows, cols] = scaled
                    dot_q[c] = dot_q[c] + value
                else:
                    gk_sum = gk_sum + line
                    sk[rows, cols] = scaled
                    dot_k[c] = dot_k[c] + value
        gain_lines.append(jnp.concatenate([gq_sum, gk_sum, jnp.zeros((6, HD), F32)], axis=0))
    gains[...] = jnp.concatenate(gain_lines, axis=1)
    lines = [to_row(jnp.concatenate(x, axis=0)) for x in (dot_q, dot_k)]
    dots[...] = jnp.concatenate(lines + [jnp.zeros((6, total), F32)], axis=0)


def project_back_body(members, planes, idx, sq, sk, dv, q0, k0, a, *refs):
    squares, dots = refs[:members], refs[members : 2 * members]
    d3, keep, away = refs[2 * members :]
    md = idx[2]
    total, own = q0.shape
    inv = inverse_rms(squares)
    mean = dots[0][...]
    for d in dots[1:]:
        mean = mean + d[...]
    mean = mean / D
    for c in range(0, total, 128):
        rows = slice(c, c + 128)
        for i, (scaled, raw) in enumerate(((sq, q0), (sk, k0))):
            col = to_column(inv[i : i + 1, c : c + 128])
            avg = to_column(mean[i : i + 1, c : c + 128])
            unit = raw[rows, :] * col
            d3[rows, i * own : (i + 1) * own] = ((scaled[rows, :] - unit * avg) * col).astype(BF16)
    d3[:, 2 * own :] = dv[...]
    half = own // 2
    for out, side in ((away, 1 - md), (keep, md)):
        for s in range(members):
            cols = pl.ds(pl.multiple_of(s * own + side * half, half), half)
            out[s * half : (s + 1) * half, :] = dot_tn(a[:, cols], d3[...]).astype(out.dtype)


def input_back_body(members, idx, d3, w, *outs):
    me = idx[0]
    length = outs[0].shape[0]
    for k in list(range(1, members)) + [0]:
        rows = pl.ds(pl.multiple_of((me ^ k) * length, length), length)
        outs[k][...] = dot_nt(d3[rows, :], w[...]).astype(outs[k].dtype)


def input_body(members, experts, idx, own, *refs):
    got, sms = refs[: members - 1], refs[members - 1 : 2 * members - 1]
    hidden, grad, out, line, gain = refs[2 * members - 1 :]
    place_gain(members, experts, hidden.shape[0], 0, idx, sms, gain)
    total = own[...]
    for g in got:
        total = total + g[...].astype(F32)
    h = hidden[...].astype(F32)
    inv = lax.rsqrt(jnp.mean(h * h, axis=-1, keepdims=True) + EPSILON)
    unit = h * inv
    line[...] = jnp.broadcast_to(jnp.sum(total * unit, axis=0, keepdims=True), line.shape)
    scaled = total * gain[...]
    out[...] = grad[...] + (scaled - unit * jnp.mean(scaled * unit, axis=-1, keepdims=True)) * inv


def output_grad_body(members, idx, mixed, *refs):
    pieces, (keep, away, grads, sems) = refs[:members], refs[members:]
    me, md = idx[0], idx[2]
    length, half = pieces[0].shape[0], keep.shape[0]
    pairs = []
    for k in range(members):
        rows = pl.ds(pl.multiple_of((me ^ k) * length, length), length)
        pairs.append((pieces[k], grads.at[rows]))
    copy_all(pairs, sems)
    for out, side in ((away, 1 - md), (keep, md)):
        cols = pl.ds(pl.multiple_of(side * half, half), half)
        out[...] = dot_tn(mixed[:, cols], grads[...]).astype(out.dtype)


def split_body(planes, parts, idx, keep, peer, *outs):
    mz = idx[1]
    slab = keep.shape[0] // (parts * planes)
    for j in range(planes):
        z = lax.rem(mz + j, planes)
        for p in range(parts):
            rows = pl.ds(pl.multiple_of((p * planes + z) * slab, slab), slab)
            value = keep[rows, :] + peer[rows, :].astype(F32)
            outs[j][p * slab : (p + 1) * slab, :] = value.astype(outs[j].dtype)


def add_body(members, idx, *refs):
    values, outs = refs[: len(refs) - members], refs[len(refs) - members :]
    me = idx[0]
    slab = outs[0].shape[0]
    for k in range(members):
        rows = pl.ds(pl.multiple_of((me ^ k) * slab, slab), slab) if members > 1 else slice(0, slab)
        total = values[0][rows, :]
        for value in values[1:]:
            total = total + value[rows, :].astype(F32)
        outs[k][...] = total.astype(BF16)


def merge_body(members, idx, *refs):
    pieces, out = refs[:members], refs[members]
    me = idx[0]
    own = pieces[0].shape[1] // 3
    for k in range(members):
        for i in range(3):
            cols = pl.ds(pl.multiple_of(i * members * own + (me ^ k) * own, own), own)
            out[:, cols] = pieces[k][:, i * own : (i + 1) * own]


def spread_body(planes, idx, *refs):
    pieces, outs = refs[: 2 * planes], refs[2 * planes :]
    mz, md = idx[1], idx[2]
    slab = pieces[0].shape[0]
    width = outs[0].shape[1]
    for c in range(2):
        side = md if c == 0 else 1 - md
        for j in range(planes):
            row = side * (planes * slab) + lax.rem(mz + j, planes) * slab
            rows = pl.ds(pl.multiple_of(row, slab), slab)
            for i, out in enumerate(outs):
                out[rows, :] = pieces[c * planes + j][:, i * width : (i + 1) * width].astype(F32)


def shards(
    hidden_in,
    grad_out,
    doc_lengths,
    expert_ids,
    attn_gain,
    query_gain,
    key_gain,
    mlp_gain,
    w_query,
    w_key,
    w_value,
    w_output,
    w_router,
    w_gate,
    w_up,
    w_down,
):
    length = hidden_in.shape[0]
    members = lax.axis_size("shard")
    planes = lax.axis_size("expert")
    me = lax.axis_index("shard")
    mz = lax.axis_index("expert")
    md = lax.axis_index("dp")
    total = length * members
    experts = planes * members
    capacity = 5 * length * TOP // (4 * experts)
    own = D // members
    local_heads = HEADS // members
    scale = HD ** (-0.5)
    others = range(1, members)

    def swap(value, k):
        return lax.ppermute(value, "shard", [(i, i ^ k) for i in range(members)])

    def fetch_z(value, j):
        return lax.ppermute(value, "expert", [(i, (i - j) % planes) for i in range(planes)])

    def return_z(value, j):
        return lax.ppermute(value, "expert", [(i, (i + j) % planes) for i in range(planes)])

    def swap_dp(value):
        return lax.ppermute(value, "dp", [(0, 1), (1, 0)])

    def exchange(pieces):
        return [pieces[0]] + [swap(pieces[k], k) for k in others]

    def gate(values, others):
        return list(lax.optimization_barrier((*values, *others))[: len(values)])

    def gather_plane(value):
        return exchange([value] * members)

    def gather_z(value):
        return [value] + [fetch_z(value, j) for j in range(1, planes)]

    idx = jnp.stack([me, mz, md]).astype(jnp.int32)
    half = own // 2
    slab = half // planes
    inner = w_gate.shape[2]
    slots = (capacity + 3 + 15) // 16 * 16
    rows = members * slots
    whole = planes * rows

    router_rows = experts // members
    extra = w_router.T.reshape(members, router_rows, own).transpose(1, 0, 2).reshape(router_rows, D)
    gains = jnp.concatenate([attn_gain, mlp_gain, jnp.zeros((D - 2 * own,), BF16)])[None]
    extra = jnp.concatenate([extra, gains], axis=0)
    extra = jnp.pad(extra, ((0, -extra.shape[0] % 16), (0, 0)))
    small = gather_plane(jnp.concatenate([hidden_in, extra], axis=0))

    def prepare(choice, after=()):
        return call(
            functools.partial(prepare_body, choice, members),
            (idx, w_query, w_key, w_value),
            "svvv",
            [((half, 3 * own), BF16)] * len(choice),
            after=after,
        )

    last = members - 1
    sent = prepare(range(1, last)) + prepare([last], small[1:2])
    got = [swap(sent[k - 1], k) for k in others]
    peers = [swap_dp(g) for g in got]

    doc_ids, doc_place = doc_layout(doc_lengths[0], total)
    cosine, sine = rope_tables(doc_place)
    sine = jnp.concatenate([-sine[:, : HD // 2], sine[:, HD // 2 :]], axis=1)
    gain_query, gain_key = query_gain[None], key_gain[None]

    hit = jnp.any(expert_ids[:, :, None] == jnp.arange(experts, dtype=jnp.int32), axis=1)
    before = jnp.triu(jnp.ones((length, length), BF16))
    rank = dot(hit.T.astype(BF16), before) - 1.0
    place = jnp.pad(jnp.where(hit.T, rank, -1.0).astype(BF16), ((0, 0), (0, D - length)))
    grads_z = lax.all_gather(jnp.concatenate([grad_out, place], axis=0), "expert")
    places = grads_z[:, length:, :length].astype(F32)

    query_raw, key_raw, value_rows, attn_input, w_qkv, squares = call(
        functools.partial(project_body, members, experts),
        (idx, *small, w_query, w_key, w_value, *got, *peers),
        "s" + "v" * members + "a" * (1 + 2 * members),
        [
            ((total, own), F32),
            ((total, own), F32),
            ((total, own), BF16),
            ((total, D), BF16),
            ((D, 3 * own), BF16),
            ((8, total), F32),
        ],
        scratch=[pltpu.VMEM((1, D), F32), pltpu.SemaphoreType.DMA((1 + 2 * members,))],
        after=[cosine, sine, places],
    )
    squares = gather_plane(squares)

    def dispatch(source, blocks, gated, after=()):
        return call(
            functools.partial(dispatch_body, blocks, gated, members, planes, capacity, slots),
            (idx, places, source),
            "sva",
            [((len(blocks) * slots, D), BF16)] * members,
            scratch=[
                pltpu.VMEM((len(blocks), length + experts, D), BF16),
                pltpu.SemaphoreType.DMA((len(blocks),)),
            ],
            after=after,
        )

    first_sent = dispatch(grads_z, [0], False, [value_rows])
    first_grads = exchange(gate(first_sent, squares[1:]))
    weights = [w_gate[0], w_up[0], w_down[0]]
    weights = [w for pair in zip(weights, map(swap_dp, gate(weights, squares[1:]))) for w in pair]
    result = call(
        functools.partial(attend_body, members, scale),
        (idx, doc_lengths, query_raw, key_raw, value_rows, *squares, cosine, sine, gain_query, gain_key, w_output),
        "ss" + "d" * (8 + members),
        [((length, D), F32)]
        + [((length, D), BF16)] * (members - 1)
        + [((total, own), BF16)] * 3
        + [((total, 128), F32)],
        after=first_sent[:1],
    )
    partial = exchange(gate(result[:members], first_grads[1:]))
    query_heads, key_heads, mixed, log_total = result[members:]
    residual, packed, route = call(
        functools.partial(route_body, members, experts),
        (idx, hidden_in, *partial, *small),
        "s" + "v" * (1 + 2 * members),
        [((length, D), F32), ((length + experts, D), BF16), ((experts, length), F32)],
        scratch=[pltpu.VMEM((experts, D), F32), pltpu.VMEM((1, D), F32)],
        after=weights[1::2],
    )

    input_z = lax.all_gather(packed, "expert")
    turns = list(range(1, planes)) + [0]
    chunks = [turns[: planes // 2], turns[planes // 2 :]]
    spot = {j: (c, i) for c, chunk in enumerate(chunks) for i, j in enumerate(chunk)}
    other_grads = exchange(dispatch(grads_z, turns[:-1], False, [residual]))
    grad_rows = first_grads + other_grads
    grad_spot = {j: (1, (j - 1) * slots) if j else (0, 0) for j in turns}
    slot_rows, arrived, after = [], other_grads[1:], ()
    for chunk in chunks:
        sent = dispatch(input_z, chunk, True, after)
        after = sent[:1]
        slot_rows.append(exchange(gate(sent, arrived)))
        arrived = slot_rows[-1][1:]
    blocks_gm, blocks_dz, blocks_du, back = [], [], [], []
    after = ()
    for c, chunk in enumerate(chunks):
        size = len(chunk) * rows
        result = call(
            functools.partial(expert_body, [grad_spot[j] for j in chunk], members, capacity, slots),
            (idx, *slot_rows[c], *grad_rows, *weights),
            "s" + "a" * (3 * members + 6),
            [((len(chunk) * slots, D), BF16)] * members + [((size, inner), BF16)] * 3,
            scratch=[
                pltpu.VMEM((size, D), BF16),
                pltpu.VMEM((size, D), BF16),
                pltpu.VMEM((D, inner), BF16),
                pltpu.VMEM((D, inner), BF16),
                pltpu.VMEM((2, inner, D // 2), BF16),
                pltpu.SemaphoreType.DMA((2 * members * len(chunk) + 6,)),
            ],
            vmem=58,
            after=after,
        )
        after = result[:1]
        back.append(exchange(gate(result[:members], arrived)))
        arrived = back[-1][1:]
        for blocks, block in zip((blocks_gm, blocks_dz, blocks_du), result[members:]):
            blocks.append(block)

    def collect(j, pieces, first, graded, after=()):
        outs = [((length + (16 if graded and j > 0 else 0), D), F32 if j == 0 else BF16)]
        if graded and j == 0:
            outs.append(((16, length), F32))
        return call(
            functools.partial(collect_body, j, first, graded, j > 0, members, planes, capacity, slots),
            (idx, places, *pieces),
            "sv" + "a" * members,
            outs,
            scratch=[
                pltpu.VMEM((rows, D), BF16),
                pltpu.VMEM((rows, length), BF16),
                pltpu.SemaphoreType.DMA((members,)),
            ],
            after=after,
        )

    order = [(j, k) for j in turns for k in range(members)]
    row_spot = [(spot[j][0] * members + k, spot[j][1] * slots) for j, k in order]
    grads_spot = [(grad_spot[j][0] * members + k, grad_spot[j][1]) for j, k in order]

    def weight_grad(body, where, pieces, blocks, shape, after):
        return call(
            functools.partial(body, where, slots),
            (idx, *pieces, *blocks),
            "s" + "a" * (len(pieces) + len(blocks)),
            [(shape, F32), (shape, BF16)],
            scratch=[
                pltpu.VMEM((whole, D), BF16),
                pltpu.VMEM((whole, inner), BF16),
                pltpu.SemaphoreType.DMA((len(where) + len(blocks),)),
            ],
            vmem=48,
            after=after,
        )

    def outputs(blocks, after):
        return call(
            functools.partial(down_body, [(spot[j][0], spot[j][1] * rows) for j in blocks], members, slots),
            (idx, *blocks_gm, *weights[4:]),
            "s" + "v" * 4,
            [((len(blocks) * slots, D), BF16)] * members,
            after=after,
        )

    all_rows = [piece for pieces in slot_rows for piece in pieces]
    quarter = planes // 4
    out_chunks = [turns[:quarter], turns[quarter : 2 * quarter], turns[2 * quarter : -1], [0]]
    sums, after = {}, ()
    for j in chunks[0]:
        sums[j] = collect(j, back[spot[j][0]], spot[j][1] * slots, True, after)
        after = sums[j][:1]
    half_d = D // 2
    gate_part = weight_grad(row_grad_body, row_spot, all_rows, blocks_dz, (half_d, inner), after)
    up_part = weight_grad(row_grad_body, row_spot, all_rows, blocks_du, (half_d, inner), gate_part[:1])
    first_out = outputs(out_chunks[0], up_part[:1])
    after = first_out[:1]
    for j in chunks[1]:
        sums[j] = collect(j, back[spot[j][0]], spot[j][1] * slots, True, after)
        after = sums[j][:1]
    later_out = [outputs(chunk, after) for chunk in out_chunks[1:]]
    first_out = exchange(gate(first_out, back[1][1:]))
    returned = [return_z(sums[j][0], j) for j in range(1, planes)]
    grad_residual, grad_low, small_part = call(
        functools.partial(token_body, members, planes, experts),
        (idx, *sums[0], *returned, route, residual, packed, grad_out, *small),
        "s" + "v" * (2 + planes - 1 + 4 + members),
        [((length, D), F32), ((length, D), BF16), ((experts + 8, D), F32)],
        scratch=[pltpu.VMEM((experts, D), F32), pltpu.VMEM((1, D), F32)],
        after=[*first_out[1:], *(out[0] for out in later_out)],
    )
    grad_all = gather_plane(grad_low)
    def token_sums(c, pieces, after=()):
        return [collect(j, pieces, i * slots, False, after)[0] for i, j in enumerate(out_chunks[c])]

    def returns(c, values):
        return [return_z(value, j) for j, value in zip(out_chunks[c], values)]

    out_sums = token_sums(0, first_out)
    out_parts = returns(0, out_sums)

    output_keep, output_away = call(
        functools.partial(output_grad_body, members),
        (idx, mixed, *grad_all),
        "sv" + "a" * members,
        [((half, D), F32), ((half, D), BF16)],
        scratch=[pltpu.VMEM((total, D), BF16), pltpu.SemaphoreType.DMA((members,))],
        after=out_sums,
    )
    output_peer = swap_dp(output_away)
    middle_out = exchange(gate(later_out[0], grad_all[1:]))
    out_sums = token_sums(1, middle_out)

    def split_z(keep, peer, parts, after=()):
        height, width = keep.shape
        return call(
            functools.partial(split_body, planes, parts),
            (idx, keep, peer),
            "svv",
            [((height // planes, width), F32)] + [((height // planes, width), BF16)] * (planes - 1),
            after=after,
        )

    def scatter_z(pieces):
        return [pieces[0]] + [return_z(pieces[j], j) for j in range(1, planes)]

    def add_z(pieces, holders, after=()):
        height, width = pieces[0].shape
        return call(
            functools.partial(add_body, holders),
            (idx, *pieces),
            "s" + "v" * planes,
            [((height // holders, width), BF16)] * holders,
            after=after,
        )

    def spread_z(pieces, count):
        pieces = pieces + [swap_dp(p) for p in pieces]
        return call(
            functools.partial(spread_body, planes),
            (idx, *pieces),
            "s" + "v" * (2 * planes),
            [((own, D), F32)] * count,
        )

    grad_value, scaled_query, scaled_key, dots, grad_gains = call(
        functools.partial(attend_back_body, members, scale),
        (
            idx,
            doc_lengths,
            *grad_all,
            *squares,
            w_output,
            query_heads,
            key_heads,
            value_rows,
            log_total,
            query_raw,
            key_raw,
            cosine,
            sine,
            gain_query,
            gain_key,
        ),
        "ss" + "a" * members + "d" * (members + 11),
        [
            ((total, own), BF16),
            ((total, own), F32),
            ((total, own), F32),
            ((8, total), F32),
            ((8, own), F32),
        ],
        scratch=[
            pltpu.VMEM((total, D), BF16),
            pltpu.VMEM((total, own), BF16),
            pltpu.VMEM((total, HD), F32),
            pltpu.VMEM((total, HD), F32),
            pltpu.SemaphoreType.DMA((members,)),
        ],
        after=[output_keep],
    )
    dots = gather_plane(dots)
    output_piece = add_z(scatter_z(split_z(output_keep, output_peer, 1, [grad_value])), 1)[0]

    grad_raw, keep, away = call(
        functools.partial(project_back_body, members, planes),
        (idx, scaled_query, scaled_key, grad_value, query_raw, key_raw, attn_input, *squares, *dots),
        "s" + "d" * (6 + 2 * members),
        [((total, 3 * own), BF16), ((D // 2, 3 * own), F32), ((D // 2, 3 * own), BF16)],
        vmem=48,
        after=[*out_parts, *out_sums],
    )

    partial_sent = call(
        functools.partial(input_back_body, members),
        (idx, grad_raw, w_qkv),
        "svv",
        [((length, D), F32)] + [((length, D), BF16)] * (members - 1),
    )

    out_parts += returns(1, out_sums)
    third_out = exchange(gate(later_out[1], dots[1:]))
    third_sums = token_sums(2, third_out)
    split = split_z(keep, swap_dp(away), members, [partial_sent[0], output_piece])
    partial_sent = gate(partial_sent, split[1:2])
    scattered = scatter_z(split)
    summed = add_z(scattered, members, third_sums)
    summed = exchange(summed)
    piece = call(
        functools.partial(merge_body, members),
        (idx, *summed),
        "s" + "v" * members,
        [((slab, 3 * D), BF16)],
    )[0]
    output_pieces = gather_z(gate([output_piece], [piece])[0])
    out_parts += returns(2, third_sums)
    down_part = weight_grad(
        col_grad_body, grads_spot, grad_rows, blocks_gm, (inner, half_d), [piece]
    )
    away = [*gate([gate_part[1], up_part[1]], [piece]), down_part[1]]
    grad_gate, grad_up, grad_down = (
        (part[0] + swap_dp(peer).astype(F32))[None]
        for part, peer in zip((gate_part, up_part, down_part), away)
    )
    partial = exchange(partial_sent)
    last_out = exchange(gate(later_out[2], partial[1:]))
    last_sums = token_sums(3, last_out)
    block_out = residual + last_sums[0]
    for part in out_parts:
        block_out = block_out + part.astype(F32)
    block_out = block_out.astype(BF16)
    grad_in, line = call(
        functools.partial(input_body, members, experts),
        (idx, *partial, *small, hidden_in, grad_residual),
        "s" + "v" * (2 * members + 2),
        [((length, D), F32), ((8, D), F32)],
        scratch=[pltpu.VMEM((1, D), F32)],
        after=[piece],
    )

    small_part = jnp.concatenate([small_part[: experts + 1], line[:1]], axis=0)
    small_pieces = small_part.reshape(experts + 2, members, own).transpose(1, 0, 2)
    small_sum = at(small_pieces, me)
    for k in others:
        small_sum = small_sum + swap(at(small_pieces, me ^ k), k)
    small_sum = jnp.concatenate([small_sum, grad_gains[:2]], axis=0)
    small_sum = small_sum + swap_dp(small_sum)
    stack = jnp.stack(gather_z(small_sum))
    small_total = at(stack, (0 - mz) % planes)
    for z in range(1, planes):
        small_total = small_total + at(stack, (z - mz) % planes)
    output_sum = spread_z(output_pieces, 1)[0]
    grad_query, grad_key, grad_value_w = spread_z(gather_z(piece), 3)

    return (
        block_out,
        grad_in,
        small_total[experts + 1],
        small_total[experts + 2],
        small_total[experts + 3],
        small_total[experts],
        grad_query,
        grad_key,
        grad_value_w,
        output_sum,
        small_total[:experts].T,
        grad_gate,
        grad_up,
        grad_down,
    )


def solution(mesh):
    return jax.shard_map(
        shards,
        mesh=mesh,
        in_specs=(
            P(("dp", "expert", "shard"), None),
            P(("dp", "expert", "shard"), None),
            P(("dp", "expert"), None),
            P(("dp", "expert", "shard"), None),
            P("shard"),
            P("shard"),
            P("shard"),
            P("shard"),
            P("shard", None),
            P("shard", None),
            P("shard", None),
            P("shard", None),
            P("shard", None),
            P(("expert", "shard"), "dp", None),
            P(("expert", "shard"), "dp", None),
            P(("expert", "shard"), None, "dp"),
        ),
        out_specs=(
            P(("dp", "expert", "shard"), None),
            P(("dp", "expert", "shard"), None),
            P("shard"),
            P("shard"),
            P("shard"),
            P("shard"),
            P("shard", None),
            P("shard", None),
            P("shard", None),
            P("shard", None),
            P("shard", None),
            P(("expert", "shard"), "dp", None),
            P(("expert", "shard"), "dp", None),
            P(("expert", "shard"), None, "dp"),
        ),
        check_vma=False,
    )
```

```python
import functools
import math

import jax
import jax.numpy as jnp
from jax import lax
from jax.experimental import pallas as pl
from jax.experimental.pallas import tpu as pltpu
from jax.sharding import PartitionSpec as P

D = 2048
HEADS = 16
HD = 128
TOP = 8
DOCS = 4

EPSILON = 1e-05
ROPE_BASE = 10000.0
NEG_FILL = -1e30

F32 = jnp.float32
BF16 = jnp.bfloat16


def dot(a, b):
    return jnp.dot(a, b, preferred_element_type=F32)


def dot_nt(a, b):
    return lax.dot_general(a, b, (((1,), (1,)), ((), ())), preferred_element_type=F32)


def dot_tn(a, b):
    return lax.dot_general(a, b, (((0,), (0,)), ((), ())), preferred_element_type=F32)


def at(stack, index):
    return lax.dynamic_index_in_dim(stack, index, 0, keepdims=False)


def doc_layout(lengths, total):
    doc_ends = jnp.cumsum(lengths)
    doc_starts = doc_ends - lengths
    places = jnp.arange(total, dtype=jnp.int32)
    doc_ids = jnp.sum((places[:, None] >= doc_ends[None, :]).astype(jnp.int32), axis=1)
    owner = doc_ids[:, None] == jnp.arange(DOCS, dtype=jnp.int32)[None, :]
    begins = jnp.sum(jnp.where(owner, doc_starts[None, :], 0), axis=1)
    return doc_ids, places - begins


def rope_tables(doc_place):
    half_size = HD // 2
    freqs = jnp.exp(-math.log(ROPE_BASE) * 2.0 * jnp.arange(half_size, dtype=F32) / HD)
    angles = doc_place.astype(F32)[:, None] * freqs
    angles = jnp.concatenate([angles, angles], axis=-1)
    return jnp.cos(angles), jnp.sin(angles)


PART = 256
MIB = 1024 * 1024


def call(body, args, kinds, outs, scratch=(), vmem=40, after=()):
    spaces = {"v": pltpu.VMEM, "s": pltpu.SMEM, "a": pl.ANY, "d": pl.ANY}
    count, moved = len(args), [i for i, kind in enumerate(kinds) if kind == "d"]
    extra = [pltpu.VMEM(args[i].shape, args[i].dtype) for i in moved]
    if moved:
        extra.append(pltpu.SemaphoreType.DMA((len(moved),)))

    def run(*refs):
        given, rest = list(refs[:count]), list(refs[count + len(after) :])
        if moved:
            held, sems = rest[-len(moved) - 1 : -1], rest[-1]
            rest = rest[: -len(moved) - 1]
            copy_all([(given[i], to) for i, to in zip(moved, held)], sems)
            for i, to in zip(moved, held):
                given[i] = to
        body(*given, *rest)

    return pl.pallas_call(
        run,
        out_shape=[jax.ShapeDtypeStruct(shape, dtype) for shape, dtype in outs],
        in_specs=[pl.BlockSpec(memory_space=spaces[kind]) for kind in kinds + "a" * len(after)],
        out_specs=[pl.BlockSpec(memory_space=pltpu.VMEM) for _ in outs],
        scratch_shapes=[*scratch, *extra],
        compiler_params=pltpu.CompilerParams(vmem_limit_bytes=vmem * MIB),
        cost_estimate=pl.CostEstimate(flops=1000, bytes_accessed=1000, transcendentals=0),
    )(*args, *after)


def copy_all(pairs, sems):
    copies = [pltpu.make_async_copy(a, b, sems.at[i]) for i, (a, b) in enumerate(pairs)]
    for c in copies:
        c.start()
    for c in copies:
        c.wait()


def iota(shape, axis):
    return lax.broadcasted_iota(jnp.int32, shape, axis)


def split3(x):
    hi = x.astype(BF16).astype(F32)
    mid = (x - hi).astype(BF16).astype(F32)
    lo = (x - hi - mid).astype(BF16).astype(F32)
    return hi, mid, lo


def pick_rows(place, slots):
    slot = iota((slots, place.shape[1]), 0).astype(F32)
    return jnp.where(slot == place, 1.0, 0.0).astype(BF16)


def dispatch_body(shifts, gated, members, planes, capacity, slots, idx, places, source, *refs):
    outs, (rows, sems) = refs[:members], refs[members:]
    experts, length = places.shape[1:]
    me, mz = idx[0], idx[1]
    copies = []
    for n, shift in enumerate(shifts):
        z = lax.rem(mz + shift, planes)
        block = source.at[z] if len(source.shape) == 3 else source
        copies.append(pltpu.make_async_copy(block, rows.at[n], sems.at[n]))
    for copy in copies:
        copy.start()
    for n, shift in enumerate(shifts):
        z = lax.rem(mz + shift, planes)
        span = slice(n * slots, (n + 1) * slots)
        copies[n].wait()
        for k in range(members):
            expert = mz * members + (me ^ k)
            pick = pick_rows(places[z, pl.ds(expert, 1), :], slots)
            result = dot(pick, rows[n, 0:length, :])
            outs[k][span, :] = result.astype(BF16)
            if gated:
                head = result[:, 0:128]
                row = iota((slots, 128), 0)
                for part in range(3):
                    table = rows[n, length : length + experts, part * PART : part * PART + length].astype(F32)
                    gate = jnp.sum(jnp.where(iota(table.shape, 0) == expert, table, 0.0), axis=0, keepdims=True)
                    gate = jnp.broadcast_to(gate, (8, length)).astype(BF16)
                    slot = dot_nt(gate, pick)[0:1, :]
                    if slots < 128:
                        slot = jnp.concatenate([slot, jnp.zeros((1, 128 - slots), F32)], axis=1)
                    head = head + jnp.where(row == capacity + part, slot, 0.0)
                outs[k][span, 0:128] = head.astype(BF16)


def expert_body(where, members, capacity, slots, idx, *refs):
    groups = 1 + max(g for g, _ in where)
    xs, cs = refs[:members], refs[members : members + groups * members]
    refs = refs[members + groups * members :]
    weights, rest = refs[:6], refs[6:]
    ds, (gm, dz, du) = rest[:members], rest[members : members + 3]
    x, c, wg, wu, wd, sems = rest[members + 3 :]
    md = idx[2]
    half = wd.shape[2]
    pairs = []
    pieces = [(i, k) for i in range(len(where)) for k in range(members)]
    for n, (i, k) in enumerate(pieces):
        g, first = where[i]
        to = pl.ds(n * slots, slots)
        pairs.append((xs[k].at[pl.ds(i * slots, slots)], x.at[to]))
        pairs.append((cs[g * members + k].at[pl.ds(first, slots)], c.at[to]))
    for n, side in ((0, md), (1, 1 - md)):
        rows = pl.ds(pl.multiple_of(side * half, half), half)
        pairs += [(weights[n], wg.at[rows]), (weights[2 + n], wu.at[rows])]
        pairs.append((weights[4 + n], wd.at[side]))
    copy_all(pairs, sems)
    inner = wg.shape[1]
    rows = len(pieces) * slots
    eye = iota((slots, 128), 0) == iota((slots, 128), 1)
    row = iota((slots, 128), 0)
    gates = []
    for n in range(len(pieces)):
        part = x[n * slots : (n + 1) * slots, 0:128].astype(F32)
        line = jnp.sum(
            jnp.where((row >= capacity) & (row < capacity + 3), part, 0.0), axis=0, keepdims=True
        )
        gates.append(jnp.sum(jnp.where(eye, line, 0.0), axis=1, keepdims=True))
    gate = jnp.concatenate(gates, axis=0)
    gate_grad = jnp.zeros((rows, 1), F32)
    step = 256 if rows <= 1024 else 128
    for n in range(0, inner, step):
        cols = slice(n, n + step)
        z = dot(x[...], wg[:, cols])
        u = dot(x[...], wu[:, cols])
        raw = dot_nt(c[:, 0:half], wd[0, cols, :]) + dot_nt(c[:, half:], wd[1, cols, :])
        sig = 1.0 / (1.0 + jnp.exp(-z))
        silu = z * sig
        middle = silu * u
        gate_grad = gate_grad + jnp.sum(
            raw * middle.astype(BF16).astype(F32), axis=1, keepdims=True
        )
        gm[:, cols] = (gate * middle).astype(BF16)
        raw = raw * gate
        dz[:, cols] = (raw * u * sig * (1.0 + z * (1.0 - sig))).astype(BF16)
        du[:, cols] = (raw * silu).astype(BF16)
    for n in range(0, wg.shape[0], 2 * step):
        cols = slice(n, n + 2 * step)
        result = dot_nt(dz[...], wg[cols, :]) + dot_nt(du[...], wu[cols, :])
        for m, (i, k) in enumerate(pieces):
            ds[k][i * slots : (i + 1) * slots, cols] = result[m * slots : (m + 1) * slots].astype(BF16)
    for m, (i, k) in enumerate(pieces):
        span = slice(i * slots, (i + 1) * slots)
        col = gate_grad[m * slots : (m + 1) * slots]
        line = jnp.sum(jnp.where(eye, col, 0.0), axis=0, keepdims=True)
        head = ds[k][span, 0:128].astype(F32)
        for part, value in enumerate(split3(line)):
            head = head + jnp.where(row == capacity + part, value, 0.0)
        ds[k][span, 0:128] = head.astype(BF16)


def collect_body(shift, first, graded, low, members, planes, capacity, slots, idx, places, *refs):
    rows, outs, (stack, pick, sems) = refs[:members], refs[members:-3], refs[-3:]
    length = places.shape[2]
    me, mz = idx[0], idx[1]
    z = lax.rem(mz + shift, planes)
    copies = [
        pltpu.make_async_copy(rows[k].at[pl.ds(first, slots)], stack.at[pl.ds(k * slots, slots)], sems.at[k])
        for k in range(members)
    ]
    for copy in copies:
        copy.start()
    for k in range(members):
        expert = mz * members + (me ^ k)
        pick[k * slots : (k + 1) * slots, :] = pick_rows(places[z, pl.ds(expert, 1), :], slots)
    for copy in copies:
        copy.wait()
    out = outs[0]
    result = dot_tn(pick[...], stack[...])
    out[0:length, :] = result.astype(out.dtype)
    if not graded:
        return
    slab = iota((16, length), 0)
    lines = jnp.zeros((16, length), F32)
    row = iota((slots, 128), 0)
    for k in range(members):
        head = stack[k * slots : (k + 1) * slots, 0:128].astype(F32)
        pieces = [
            jnp.sum(jnp.where(row == capacity + i, head, 0.0), axis=0, keepdims=True) for i in range(3)
        ]
        pieces = jnp.concatenate(pieces + [jnp.zeros((5, 128), F32)], axis=0).astype(BF16)
        line = jnp.sum(
            dot(pieces[:, 0:slots], pick[k * slots : (k + 1) * slots, :]), axis=0, keepdims=True
        )
        lines = lines + jnp.where(slab == (me ^ k), line, 0.0)
    if low:
        out[length : length + 16, :] = jnp.zeros((16, out.shape[1]), BF16)
        for i, value in enumerate(split3(lines)):
            out[length : length + 16, i * PART : i * PART + length] = value.astype(BF16)
    else:
        outs[1][...] = lines


def load_pieces(where, arrays, slots, out):
    return [
        (arrays[g].at[pl.ds(first, slots)], out.at[pl.ds(i * slots, slots)])
        for i, (g, first) in enumerate(where)
    ]


def load_blocks(blocks, out):
    pairs, first = [], 0
    for block in blocks:
        pairs.append((block, out.at[pl.ds(first, block.shape[0])]))
        first += block.shape[0]
    return pairs


def row_grad_body(where, slots, idx, *refs):
    count = 1 + max(g for g, _ in where)
    pieces, blocks = refs[:count], refs[count:-5]
    keep, away, a, b, sems = refs[-5:]
    copy_all(load_pieces(where, pieces, slots, a) + load_blocks(blocks, b), sems)
    md = idx[2]
    step, half = 256, keep.shape[0]
    for out, side in ((away, 1 - md), (keep, md)):
        for n in range(0, half, step):
            cols = pl.ds(pl.multiple_of(side * half + n, step), step)
            out[n : n + step, :] = dot_tn(a[:, cols], b[...]).astype(out.dtype)


def col_grad_body(where, slots, idx, *refs):
    count = 1 + max(g for g, _ in where)
    pieces, blocks = refs[:count], refs[count:-5]
    keep, away, b, a, sems = refs[-5:]
    copy_all(load_pieces(where, pieces, slots, b) + load_blocks(blocks, a), sems)
    md = idx[2]
    step, half = 256, keep.shape[1]
    for n in range(0, keep.shape[0], step):
        lhs = a[:, n : n + step]
        for out, side in ((away, 1 - md), (keep, md)):
            cols = pl.ds(pl.multiple_of(side * half, half), half)
            out[n : n + step, :] = dot_tn(lhs, b[:, cols]).astype(out.dtype)


def down_body(where, members, slots, idx, *refs):
    count = len(refs) - members - 2
    blocks, (mine, peer), outs = refs[:count], refs[count : count + 2], refs[count + 2 :]
    md = idx[2]
    half = mine.shape[1]
    rows = members * slots
    for n, (g, first) in enumerate(where):
        for w, side in ((mine, md), (peer, 1 - md)):
            cols = pl.ds(pl.multiple_of(side * half, half), half)
            result = dot(blocks[g][first : first + rows, :], w[...])
            for k in range(members):
                outs[k][n * slots : (n + 1) * slots, cols] = result[k * slots : (k + 1) * slots].astype(BF16)


def to_row(column):
    eye = iota((128, 128), 0) == iota((128, 128), 1)
    return jnp.concatenate(
        [
            jnp.sum(jnp.where(eye, column[i : i + 128], 0.0), axis=0, keepdims=True)
            for i in range(0, column.shape[0], 128)
        ],
        axis=1,
    )


def to_column(line):
    eye = iota((128, 128), 0) == iota((128, 128), 1)
    return jnp.sum(jnp.where(eye, line, 0.0), axis=1, keepdims=True)


def prepare_body(choice, members, idx, wq, wk, wv, *outs):
    me, md = idx[0], idx[2]
    half = outs[0].shape[0]
    own = wq.shape[1] // members
    rows = pl.ds(pl.multiple_of(md * half, half), half)
    for n, k in enumerate(choice):
        cols = pl.ds(pl.multiple_of((me ^ k) * own, own), own)
        for i, w in enumerate((wq, wk, wv)):
            outs[n][:, i * own : (i + 1) * own] = w[rows, cols]


def project_body(members, experts, idx, *refs):
    hs = refs[:members]
    refs = refs[members:]
    ws, got, peer = refs[:3], refs[3 : 2 + members], refs[2 + members : 1 + 2 * members]
    q0, k0, v, a, w, squares, gain, sems = refs[1 + 2 * members :]
    me, md = idx[0], idx[2]
    total = a.shape[0]
    length = total // members
    own = q0.shape[1]
    half = own // 2
    copies = []
    base = pl.multiple_of(me * own, own)
    for i in range(3):
        copies.append((ws[i].at[:, pl.ds(base, own)], w.at[pl.ds(base, own), i * own : (i + 1) * own]))
    for k in range(1, members):
        for side, source in ((md, got), (1 - md, peer)):
            row = pl.multiple_of((me ^ k) * own + side * half, half)
            copies.append((source[k - 1], w.at[pl.ds(row, half)]))
    copies = [pltpu.make_async_copy(s, d, sems.at[i]) for i, (s, d) in enumerate(copies)]
    for c in copies:
        c.start()
    place_gain(members, experts, length, 0, idx, hs, gain)
    for k in range(members):
        h = hs[k][0:length, :].astype(F32)
        inv = lax.rsqrt(jnp.mean(h * h, axis=-1, keepdims=True) + EPSILON)
        rows = pl.ds(pl.multiple_of((me ^ k) * length, length), length)
        a[rows, :] = (h * inv * gain[...]).astype(BF16)
    for c in copies:
        c.wait()
    step = 256
    sums = [[], []]
    for n in range(0, total, step):
        rows = slice(n, n + step)
        for i, out in enumerate((q0, k0)):
            raw = dot(a[rows, :], w[:, i * own : (i + 1) * own])
            out[rows, :] = raw
            sums[i].append(jnp.sum(raw * raw, axis=1, keepdims=True))
        v[rows, :] = dot(a[rows, :], w[:, 2 * own :]).astype(BF16)
    lines = [to_row(jnp.concatenate(s, axis=0)) for s in sums]
    squares[...] = jnp.concatenate(lines + [jnp.zeros((6, total), F32)], axis=0)


def doc_start(lens, first, count):
    end0 = lens[0, 0]
    end1 = end0 + lens[0, 1]
    end2 = end1 + lens[0, 2]
    at_row = iota((count, 1), 0) + first
    later = jnp.where(at_row < end2, end1, at_row)
    start = jnp.where(at_row < end0, 0, jnp.where(at_row < end1, end0, later))
    return at_row, start


def inverse_rms(squares):
    total = squares[0][...]
    for s in squares[1:]:
        total = total + s[...]
    return lax.rsqrt(total / D + EPSILON)


def attend_body(members, scale, idx, lens, q0, k0, v, *refs):
    squares, (cosine, sine, gq, gk, wo) = refs[:members], refs[members : members + 5]
    refs = refs[members + 5 :]
    outs, (qr, kr, mixed, lse) = refs[:members], refs[members:]
    me = idx[0]
    total, own = q0.shape
    inv = inverse_rms(squares)
    for n in range(0, total, 128):
        rows = slice(n, n + 128)
        cos, sin = cosine[rows, :], sine[rows, :]
        for i, (raw, gain, out) in enumerate(((q0, gq, qr), (k0, gk, kr))):
            col = to_column(inv[i : i + 1, n : n + 128])
            for h in range(0, own, HD):
                x = raw[rows, h : h + HD] * col * gain[:, h : h + HD].astype(F32)
                out[rows, h : h + HD] = (x * cos + pltpu.roll(x, HD // 2, 1) * sin).astype(BF16)
    step = 256
    for n in range(0, total, step):
        rows = slice(n, n + step)
        at_row, start = doc_start(lens, n, step)
        at_key = iota((step, n + step), 1)
        allowed = (at_key <= at_row) & (at_key >= start)
        for h in range(0, own, HD):
            cols = slice(h, h + HD)
            s = dot_nt(qr[rows, cols], kr[0 : n + step, cols]) * scale
            s = jnp.where(allowed, s, NEG_FILL)
            top = jnp.max(s, axis=-1, keepdims=True)
            p = jnp.exp(s - top)
            norm = jnp.sum(p, axis=-1, keepdims=True)
            lse[rows, h // HD : h // HD + 1] = top + jnp.log(norm)
            p = (p * (1.0 / norm)).astype(BF16)
            mixed[rows, cols] = dot(p, v[0 : n + step, cols]).astype(BF16)
    length = outs[0].shape[0]
    for k in list(range(1, members)) + [0]:
        rows = pl.ds(pl.multiple_of((me ^ k) * length, length), length)
        outs[k][...] = dot(mixed[rows, :], wo[...]).astype(outs[k].dtype)


def place_router(members, experts, length, idx, pieces, out):
    me = idx[0]
    own = out.shape[1] // members
    count = experts // members
    for k in range(members):
        cols = pl.ds(pl.multiple_of((me ^ k) * own, own), own)
        for i in range(members):
            part = pieces[k][length:, i * own : (i + 1) * own].astype(F32)
            out[i * count : (i + 1) * count, cols] = part[0:count]


def place_gain(members, experts, length, part, idx, pieces, out):
    me = idx[0]
    own = out.shape[1] // members
    row = experts // members
    for k in range(members):
        cols = pl.ds(pl.multiple_of((me ^ k) * own, own), own)
        value = pieces[k][length:, part * own : (part + 1) * own].astype(F32)
        out[:, cols] = value[row : row + 1]


def route_body(members, experts, idx, hidden, own, *refs):
    got, sms = refs[: members - 1], refs[members - 1 : 2 * members - 1]
    h1, packed, route, router, gain = refs[2 * members - 1 :]
    length = hidden.shape[0]
    place_router(members, experts, length, idx, sms, router)
    place_gain(members, experts, length, 1, idx, sms, gain)
    h = hidden[...].astype(F32) + own[...]
    for g in got:
        h = h + g[...].astype(F32)
    h1[...] = h
    inv = lax.rsqrt(jnp.mean(h * h, axis=-1, keepdims=True) + EPSILON)
    packed[0:length, :] = (h * inv * gain[...]).astype(BF16)
    logits = dot_nt(router[...].astype(BF16), packed[0:length, :])
    e = jnp.exp(logits - jnp.max(logits, axis=0, keepdims=True))
    r = e / jnp.sum(e, axis=0, keepdims=True)
    route[...] = r
    packed[length:, :] = jnp.zeros((experts, packed.shape[1]), BF16)
    for i, value in enumerate(split3(r)):
        packed[length:, i * PART : i * PART + length] = value.astype(BF16)


def token_body(members, planes, experts, idx, own, lines, *refs):
    got, (route, h1, packed, grad_out) = refs[: planes - 1], refs[planes - 1 : planes + 3]
    sms = refs[planes + 3 : planes + 3 + members]
    grad, low, small, router, gain = refs[planes + 3 + members :]
    mz = idx[1]
    length = h1.shape[0]
    place_router(members, experts, length, idx, sms, router)
    place_gain(members, experts, length, 1, idx, sms, gain)
    total = own[...]
    spread = iota((experts, length), 0)
    grad_route = jnp.zeros((experts, length), F32)
    for j in range(planes):
        if j == 0:
            part = lines[...]
        else:
            total = total + got[j - 1][0:length, :].astype(F32)
            part = sum(
                got[j - 1][length : length + 16, i * PART : i * PART + length].astype(F32) for i in range(3)
            )
        z = lax.rem(mz - j + planes, planes)
        for s in range(members):
            grad_route = grad_route + jnp.where(spread == z * members + s, part[s : s + 1], 0.0)
    r = route[...]
    dl = (r * (grad_route - jnp.sum(r * grad_route, axis=0, keepdims=True))).astype(BF16)
    total = total + dot_tn(dl, router[...].astype(BF16))
    small[0:experts, :] = dot(dl, packed[0:length, :])
    h = h1[...]
    inv = lax.rsqrt(jnp.mean(h * h, axis=-1, keepdims=True) + EPSILON)
    unit = h * inv
    small[experts : experts + 8, :] = jnp.broadcast_to(
        jnp.sum(total * unit, axis=0, keepdims=True), (8, h.shape[1])
    )
    scaled = total * gain[...]
    back = (scaled - unit * jnp.mean(scaled * unit, axis=-1, keepdims=True)) * inv
    result = grad_out[...].astype(F32) + back
    grad[...] = result
    low[...] = result.astype(BF16)


def attend_back_body(members, scale, idx, lens, *refs):
    ds, squares = refs[:members], refs[members : 2 * members]
    wo, qr, kr, v, lse, q0, k0, cosine, sine, gq, gk = refs[2 * members : 2 * members + 11]
    dv, sq, sk, dots, gains, grads, do, dkt, dvt, sems = refs[2 * members + 11 :]
    me = idx[0]
    length = ds[0].shape[0]
    total, own = q0.shape
    pairs = []
    for k in range(members):
        rows = pl.ds(pl.multiple_of((me ^ k) * length, length), length)
        pairs.append((ds[k], grads.at[rows]))
    copy_all(pairs, sems)
    step = 256
    for n in range(0, total, step):
        do[n : n + step, :] = dot_nt(grads[n : n + step, :], wo[...]).astype(BF16)
    inv = inverse_rms(squares)
    dot_q, dot_k = [0.0] * (total // 128), [0.0] * (total // 128)
    gain_lines = []
    for h in range(0, own, HD):
        cols = slice(h, h + HD)
        for n in range(0, total, step):
            rows = slice(n, n + step)
            keys = slice(0, n + step)
            at_row, start = doc_start(lens, n, step)
            at_key = iota((step, n + step), 1)
            allowed = (at_key <= at_row) & (at_key >= start)
            s = dot_nt(qr[rows, cols], kr[keys, cols]) * scale
            p = jnp.exp(jnp.where(allowed, s - lse[rows, h // HD : h // HD + 1], NEG_FILL))
            dp = dot_nt(do[rows, cols], v[keys, cols])
            delta = jnp.sum(p * dp, axis=-1, keepdims=True)
            grad_s = (p * (dp - delta)).astype(BF16)
            part_v = dot_tn(p.astype(BF16), do[rows, cols])
            part_k = dot_tn(grad_s, qr[rows, cols])
            if n == 0:
                dkt[...] = jnp.zeros(dkt.shape, F32)
                dvt[...] = jnp.zeros(dvt.shape, F32)
            dvt[keys, :] = dvt[keys, :] + part_v
            dkt[keys, :] = dkt[keys, :] + part_k
            sq[rows, cols] = dot(grad_s, kr[keys, cols]) * scale
        dv[:, cols] = dvt[...].astype(BF16)
        gq_sum, gk_sum = jnp.zeros((1, HD), F32), jnp.zeros((1, HD), F32)
        for c in range(total // 128):
            rows = slice(c * 128, c * 128 + 128)
            cos, sin = cosine[rows, :], sine[rows, :]
            for i, raw in enumerate((q0, k0)):
                g = sq[rows, cols] if i == 0 else dkt[rows, :] * scale
                g = g * cos - pltpu.roll(g, HD // 2, 1) * sin
                unit = raw[rows, cols] * to_column(inv[i : i + 1, c * 128 : c * 128 + 128])
                line = jnp.sum(g * unit, axis=0, keepdims=True)
                scaled = g * (gq if i == 0 else gk)[:, cols].astype(F32)
                value = jnp.sum(scaled * unit, axis=1, keepdims=True)
                if i == 0:
                    gq_sum = gq_sum + line
                    sq[rows, cols] = scaled
                    dot_q[c] = dot_q[c] + value
                else:
                    gk_sum = gk_sum + line
                    sk[rows, cols] = scaled
                    dot_k[c] = dot_k[c] + value
        gain_lines.append(jnp.concatenate([gq_sum, gk_sum, jnp.zeros((6, HD), F32)], axis=0))
    gains[...] = jnp.concatenate(gain_lines, axis=1)
    lines = [to_row(jnp.concatenate(x, axis=0)) for x in (dot_q, dot_k)]
    dots[...] = jnp.concatenate(lines + [jnp.zeros((6, total), F32)], axis=0)


def project_back_body(members, planes, idx, sq, sk, dv, q0, k0, a, *refs):
    squares, dots = refs[:members], refs[members : 2 * members]
    d3, keep, away = refs[2 * members :]
    md = idx[2]
    total, own = q0.shape
    inv = inverse_rms(squares)
    mean = dots[0][...]
    for d in dots[1:]:
        mean = mean + d[...]
    mean = mean / D
    for c in range(0, total, 128):
        rows = slice(c, c + 128)
        for i, (scaled, raw) in enumerate(((sq, q0), (sk, k0))):
            col = to_column(inv[i : i + 1, c : c + 128])
            avg = to_column(mean[i : i + 1, c : c + 128])
            unit = raw[rows, :] * col
            d3[rows, i * own : (i + 1) * own] = ((scaled[rows, :] - unit * avg) * col).astype(BF16)
    d3[:, 2 * own :] = dv[...]
    half = own // 2
    for out, side in ((away, 1 - md), (keep, md)):
        for s in range(members):
            cols = pl.ds(pl.multiple_of(s * own + side * half, half), half)
            out[s * half : (s + 1) * half, :] = dot_tn(a[:, cols], d3[...]).astype(out.dtype)


def input_back_body(members, idx, d3, w, *outs):
    me = idx[0]
    length = outs[0].shape[0]
    for k in list(range(1, members)) + [0]:
        rows = pl.ds(pl.multiple_of((me ^ k) * length, length), length)
        outs[k][...] = dot_nt(d3[rows, :], w[...]).astype(outs[k].dtype)


def input_body(members, experts, idx, own, *refs):
    got, sms = refs[: members - 1], refs[members - 1 : 2 * members - 1]
    hidden, grad, out, line, gain = refs[2 * members - 1 :]
    place_gain(members, experts, hidden.shape[0], 0, idx, sms, gain)
    total = own[...]
    for g in got:
        total = total + g[...].astype(F32)
    h = hidden[...].astype(F32)
    inv = lax.rsqrt(jnp.mean(h * h, axis=-1, keepdims=True) + EPSILON)
    unit = h * inv
    line[...] = jnp.broadcast_to(jnp.sum(total * unit, axis=0, keepdims=True), line.shape)
    scaled = total * gain[...]
    out[...] = grad[...] + (scaled - unit * jnp.mean(scaled * unit, axis=-1, keepdims=True)) * inv


def output_grad_body(members, idx, mixed, *refs):
    pieces, (keep, away, grads, sems) = refs[:members], refs[members:]
    me, md = idx[0], idx[2]
    length, half = pieces[0].shape[0], keep.shape[0]
    pairs = []
    for k in range(members):
        rows = pl.ds(pl.multiple_of((me ^ k) * length, length), length)
        pairs.append((pieces[k], grads.at[rows]))
    copy_all(pairs, sems)
    for out, side in ((away, 1 - md), (keep, md)):
        cols = pl.ds(pl.multiple_of(side * half, half), half)
        out[...] = dot_tn(mixed[:, cols], grads[...]).astype(out.dtype)


def split_body(planes, parts, idx, keep, peer, *outs):
    mz = idx[1]
    slab = keep.shape[0] // (parts * planes)
    for j in range(planes):
        z = lax.rem(mz + j, planes)
        for p in range(parts):
            rows = pl.ds(pl.multiple_of((p * planes + z) * slab, slab), slab)
            value = keep[rows, :] + peer[rows, :].astype(F32)
            outs[j][p * slab : (p + 1) * slab, :] = value.astype(outs[j].dtype)


def add_body(members, idx, *refs):
    values, outs = refs[: len(refs) - members], refs[len(refs) - members :]
    me = idx[0]
    slab = outs[0].shape[0]
    for k in range(members):
        rows = pl.ds(pl.multiple_of((me ^ k) * slab, slab), slab) if members > 1 else slice(0, slab)
        total = values[0][rows, :]
        for value in values[1:]:
            total = total + value[rows, :].astype(F32)
        outs[k][...] = total.astype(BF16)


def merge_body(members, idx, *refs):
    pieces, out = refs[:members], refs[members]
    me = idx[0]
    own = pieces[0].shape[1] // 3
    for k in range(members):
        for i in range(3):
            cols = pl.ds(pl.multiple_of(i * members * own + (me ^ k) * own, own), own)
            out[:, cols] = pieces[k][:, i * own : (i + 1) * own]


def spread_body(planes, idx, *refs):
    pieces, outs = refs[: 2 * planes], refs[2 * planes :]
    mz, md = idx[1], idx[2]
    slab = pieces[0].shape[0]
    width = outs[0].shape[1]
    for c in range(2):
        side = md if c == 0 else 1 - md
        for j in range(planes):
            row = side * (planes * slab) + lax.rem(mz + j, planes) * slab
            rows = pl.ds(pl.multiple_of(row, slab), slab)
            for i, out in enumerate(outs):
                out[rows, :] = pieces[c * planes + j][:, i * width : (i + 1) * width].astype(F32)


def shards(
    hidden_in,
    grad_out,
    doc_lengths,
    expert_ids,
    attn_gain,
    query_gain,
    key_gain,
    mlp_gain,
    w_query,
    w_key,
    w_value,
    w_output,
    w_router,
    w_gate,
    w_up,
    w_down,
):
    length = hidden_in.shape[0]
    members = lax.axis_size("shard")
    planes = lax.axis_size("expert")
    me = lax.axis_index("shard")
    mz = lax.axis_index("expert")
    md = lax.axis_index("dp")
    total = length * members
    experts = planes * members
    capacity = 5 * length * TOP // (4 * experts)
    own = D // members
    local_heads = HEADS // members
    scale = HD ** (-0.5)
    others = range(1, members)

    def swap(value, k):
        return lax.ppermute(value, "shard", [(i, i ^ k) for i in range(members)])

    def fetch_z(value, j):
        return lax.ppermute(value, "expert", [(i, (i - j) % planes) for i in range(planes)])

    def return_z(value, j):
        return lax.ppermute(value, "expert", [(i, (i + j) % planes) for i in range(planes)])

    def swap_dp(value):
        return lax.ppermute(value, "dp", [(0, 1), (1, 0)])

    def exchange(pieces):
        return [pieces[0]] + [swap(pieces[k], k) for k in others]

    def gate(values, others):
        return list(lax.optimization_barrier((*values, *others))[: len(values)])

    def gather_plane(value):
        return exchange([value] * members)

    def gather_z(value):
        return [value] + [fetch_z(value, j) for j in range(1, planes)]

    idx = jnp.stack([me, mz, md]).astype(jnp.int32)
    half = own // 2
    slab = half // planes
    inner = w_gate.shape[2]
    slots = (capacity + 3 + 15) // 16 * 16
    rows = members * slots
    whole = planes * rows

    router_rows = experts // members
    extra = w_router.T.reshape(members, router_rows, own).transpose(1, 0, 2).reshape(router_rows, D)
    gains = jnp.concatenate([attn_gain, mlp_gain, jnp.zeros((D - 2 * own,), BF16)])[None]
    extra = jnp.concatenate([extra, gains], axis=0)
    extra = jnp.pad(extra, ((0, -extra.shape[0] % 16), (0, 0)))
    small = gather_plane(jnp.concatenate([hidden_in, extra], axis=0))

    def prepare(choice, after=()):
        return call(
            functools.partial(prepare_body, choice, members),
            (idx, w_query, w_key, w_value),
            "svvv",
            [((half, 3 * own), BF16)] * len(choice),
            after=after,
        )

    last = members - 1
    sent = prepare(range(1, last)) + prepare([last], small[1:2])
    got = [swap(sent[k - 1], k) for k in others]
    peers = [swap_dp(g) for g in got]

    doc_ids, doc_place = doc_layout(doc_lengths[0], total)
    cosine, sine = rope_tables(doc_place)
    sine = jnp.concatenate([-sine[:, : HD // 2], sine[:, HD // 2 :]], axis=1)
    gain_query, gain_key = query_gain[None], key_gain[None]

    hit = jnp.any(expert_ids[:, :, None] == jnp.arange(experts, dtype=jnp.int32), axis=1)
    before = jnp.triu(jnp.ones((length, length), BF16))
    rank = dot(hit.T.astype(BF16), before) - 1.0
    place = jnp.pad(jnp.where(hit.T, rank, -1.0).astype(BF16), ((0, 0), (0, D - length)))
    grads_z = lax.all_gather(jnp.concatenate([grad_out, place], axis=0), "expert")
    places = grads_z[:, length:, :length].astype(F32)

    query_raw, key_raw, value_rows, attn_input, w_qkv, squares = call(
        functools.partial(project_body, members, experts),
        (idx, *small, w_query, w_key, w_value, *got, *peers),
        "s" + "v" * members + "a" * (1 + 2 * members),
        [
            ((total, own), F32),
            ((total, own), F32),
            ((total, own), BF16),
            ((total, D), BF16),
            ((D, 3 * own), BF16),
            ((8, total), F32),
        ],
        scratch=[pltpu.VMEM((1, D), F32), pltpu.SemaphoreType.DMA((1 + 2 * members,))],
        after=[cosine, sine, places],
    )
    squares = gather_plane(squares)

    def dispatch(source, blocks, gated, after=()):
        return call(
            functools.partial(dispatch_body, blocks, gated, members, planes, capacity, slots),
            (idx, places, source),
            "sva",
            [((len(blocks) * slots, D), BF16)] * members,
            scratch=[
                pltpu.VMEM((len(blocks), length + experts, D), BF16),
                pltpu.SemaphoreType.DMA((len(blocks),)),
            ],
            after=after,
        )

    first_sent = dispatch(grads_z, [0], False, [value_rows])
    first_grads = exchange(gate(first_sent, squares[1:]))
    weights = [w_gate[0], w_up[0], w_down[0]]
    weights = [w for pair in zip(weights, map(swap_dp, gate(weights, squares[1:]))) for w in pair]
    result = call(
        functools.partial(attend_body, members, scale),
        (idx, doc_lengths, query_raw, key_raw, value_rows, *squares, cosine, sine, gain_query, gain_key, w_output),
        "ss" + "d" * (8 + members),
        [((length, D), F32)]
        + [((length, D), BF16)] * (members - 1)
        + [((total, own), BF16)] * 3
        + [((total, 128), F32)],
        after=first_sent[:1],
    )
    partial = exchange(gate(result[:members], first_grads[1:]))
    query_heads, key_heads, mixed, log_total = result[members:]
    residual, packed, route = call(
        functools.partial(route_body, members, experts),
        (idx, hidden_in, *partial, *small),
        "s" + "v" * (1 + 2 * members),
        [((length, D), F32), ((length + experts, D), BF16), ((experts, length), F32)],
        scratch=[pltpu.VMEM((experts, D), F32), pltpu.VMEM((1, D), F32)],
        after=weights[1::2],
    )

    input_z = lax.all_gather(packed, "expert")
    turns = list(range(1, planes)) + [0]
    chunks = [turns[: planes // 2], turns[planes // 2 :]]
    spot = {j: (c, i) for c, chunk in enumerate(chunks) for i, j in enumerate(chunk)}
    other_grads = exchange(dispatch(grads_z, turns[:-1], False, [residual]))
    grad_rows = first_grads + other_grads
    grad_spot = {j: (1, (j - 1) * slots) if j else (0, 0) for j in turns}
    slot_rows, arrived, after = [], other_grads[1:], ()
    for chunk in chunks:
        sent = dispatch(input_z, chunk, True, after)
        after = sent[:1]
        slot_rows.append(exchange(gate(sent, arrived)))
        arrived = slot_rows[-1][1:]
    blocks_gm, blocks_dz, blocks_du, back = [], [], [], []
    after = ()
    for c, chunk in enumerate(chunks):
        size = len(chunk) * rows
        result = call(
            functools.partial(expert_body, [grad_spot[j] for j in chunk], members, capacity, slots),
            (idx, *slot_rows[c], *grad_rows, *weights),
            "s" + "a" * (3 * members + 6),
            [((len(chunk) * slots, D), BF16)] * members + [((size, inner), BF16)] * 3,
            scratch=[
                pltpu.VMEM((size, D), BF16),
                pltpu.VMEM((size, D), BF16),
                pltpu.VMEM((D, inner), BF16),
                pltpu.VMEM((D, inner), BF16),
                pltpu.VMEM((2, inner, D // 2), BF16),
                pltpu.SemaphoreType.DMA((2 * members * len(chunk) + 6,)),
            ],
            vmem=58,
            after=after,
        )
        after = result[:1]
        back.append(exchange(gate(result[:members], arrived)))
        arrived = back[-1][1:]
        for blocks, block in zip((blocks_gm, blocks_dz, blocks_du), result[members:]):
            blocks.append(block)

    def collect(j, pieces, first, graded, after=()):
        outs = [((length + (16 if graded and j > 0 else 0), D), F32 if j == 0 else BF16)]
        if graded and j == 0:
            outs.append(((16, length), F32))
        return call(
            functools.partial(collect_body, j, first, graded, j > 0, members, planes, capacity, slots),
            (idx, places, *pieces),
            "sv" + "a" * members,
            outs,
            scratch=[
                pltpu.VMEM((rows, D), BF16),
                pltpu.VMEM((rows, length), BF16),
                pltpu.SemaphoreType.DMA((members,)),
            ],
            after=after,
        )

    order = [(j, k) for j in turns for k in range(members)]
    row_spot = [(spot[j][0] * members + k, spot[j][1] * slots) for j, k in order]
    grads_spot = [(grad_spot[j][0] * members + k, grad_spot[j][1]) for j, k in order]

    def weight_grad(body, where, pieces, blocks, shape, after):
        return call(
            functools.partial(body, where, slots),
            (idx, *pieces, *blocks),
            "s" + "a" * (len(pieces) + len(blocks)),
            [(shape, F32), (shape, BF16)],
            scratch=[
                pltpu.VMEM((whole, D), BF16),
                pltpu.VMEM((whole, inner), BF16),
                pltpu.SemaphoreType.DMA((len(where) + len(blocks),)),
            ],
            vmem=48,
            after=after,
        )

    def outputs(blocks, after):
        return call(
            functools.partial(down_body, [(spot[j][0], spot[j][1] * rows) for j in blocks], members, slots),
            (idx, *blocks_gm, *weights[4:]),
            "s" + "v" * 4,
            [((len(blocks) * slots, D), BF16)] * members,
            after=after,
        )

    all_rows = [piece for pieces in slot_rows for piece in pieces]
    quarter = planes // 4
    out_chunks = [turns[quarter : 2 * quarter], turns[:quarter], turns[2 * quarter : -1], [0]]
    sums, after = {}, ()
    for j in chunks[0]:
        sums[j] = collect(j, back[spot[j][0]], spot[j][1] * slots, True, after)
        after = sums[j][:1]
    half_d = D // 2
    gate_part = weight_grad(row_grad_body, row_spot, all_rows, blocks_dz, (half_d, inner), after)
    up_part = weight_grad(row_grad_body, row_spot, all_rows, blocks_du, (half_d, inner), gate_part[:1])
    first_out = outputs(out_chunks[0], up_part[:1])
    after = first_out[:1]
    for j in chunks[1]:
        sums[j] = collect(j, back[spot[j][0]], spot[j][1] * slots, True, after)
        after = sums[j][:1]
    later_out = [outputs(chunk, after) for chunk in out_chunks[1:]]
    first_out = exchange(gate(first_out, back[1][1:]))
    returned = [return_z(sums[j][0], j) for j in range(1, planes)]
    grad_residual, grad_low, small_part = call(
        functools.partial(token_body, members, planes, experts),
        (idx, *sums[0], *returned, route, residual, packed, grad_out, *small),
        "s" + "v" * (2 + planes - 1 + 4 + members),
        [((length, D), F32), ((length, D), BF16), ((experts + 8, D), F32)],
        scratch=[pltpu.VMEM((experts, D), F32), pltpu.VMEM((1, D), F32)],
        after=[*first_out[1:], *(out[0] for out in later_out)],
    )
    grad_all = gather_plane(grad_low)
    def token_sums(c, pieces, after=()):
        return [collect(j, pieces, i * slots, False, after)[0] for i, j in enumerate(out_chunks[c])]

    def returns(c, values):
        return [return_z(value, j) for j, value in zip(out_chunks[c], values)]

    out_sums = token_sums(0, first_out)
    out_parts = returns(0, out_sums)

    output_keep, output_away = call(
        functools.partial(output_grad_body, members),
        (idx, mixed, *grad_all),
        "sv" + "a" * members,
        [((half, D), F32), ((half, D), BF16)],
        scratch=[pltpu.VMEM((total, D), BF16), pltpu.SemaphoreType.DMA((members,))],
        after=out_sums,
    )
    output_peer = swap_dp(output_away)
    middle_out = exchange(gate(later_out[0], grad_all[1:]))
    out_sums = token_sums(1, middle_out)

    def split_z(keep, peer, parts, after=()):
        height, width = keep.shape
        return call(
            functools.partial(split_body, planes, parts),
            (idx, keep, peer),
            "svv",
            [((height // planes, width), F32)] + [((height // planes, width), BF16)] * (planes - 1),
            after=after,
        )

    def scatter_z(pieces):
        return [pieces[0]] + [return_z(pieces[j], j) for j in range(1, planes)]

    def add_z(pieces, holders, after=()):
        height, width = pieces[0].shape
        return call(
            functools.partial(add_body, holders),
            (idx, *pieces),
            "s" + "v" * planes,
            [((height // holders, width), BF16)] * holders,
            after=after,
        )

    def spread_z(pieces, count):
        pieces = pieces + [swap_dp(p) for p in pieces]
        return call(
            functools.partial(spread_body, planes),
            (idx, *pieces),
            "s" + "v" * (2 * planes),
            [((own, D), F32)] * count,
        )

    grad_value, scaled_query, scaled_key, dots, grad_gains = call(
        functools.partial(attend_back_body, members, scale),
        (
            idx,
            doc_lengths,
            *grad_all,
            *squares,
            w_output,
            query_heads,
            key_heads,
            value_rows,
            log_total,
            query_raw,
            key_raw,
            cosine,
            sine,
            gain_query,
            gain_key,
        ),
        "ss" + "a" * members + "d" * (members + 11),
        [
            ((total, own), BF16),
            ((total, own), F32),
            ((total, own), F32),
            ((8, total), F32),
            ((8, own), F32),
        ],
        scratch=[
            pltpu.VMEM((total, D), BF16),
            pltpu.VMEM((total, own), BF16),
            pltpu.VMEM((total, HD), F32),
            pltpu.VMEM((total, HD), F32),
            pltpu.SemaphoreType.DMA((members,)),
        ],
        after=[output_keep],
    )
    dots = gather_plane(dots)
    output_piece = add_z(scatter_z(split_z(output_keep, output_peer, 1, [grad_value])), 1)[0]

    grad_raw, keep, away = call(
        functools.partial(project_back_body, members, planes),
        (idx, scaled_query, scaled_key, grad_value, query_raw, key_raw, attn_input, *squares, *dots),
        "s" + "d" * (6 + 2 * members),
        [((total, 3 * own), BF16), ((D // 2, 3 * own), F32), ((D // 2, 3 * own), BF16)],
        vmem=48,
        after=[*out_parts, *out_sums],
    )

    partial_sent = call(
        functools.partial(input_back_body, members),
        (idx, grad_raw, w_qkv),
        "svv",
        [((length, D), F32)] + [((length, D), BF16)] * (members - 1),
    )

    out_parts += returns(1, out_sums)
    third_out = exchange(gate(later_out[1], dots[1:]))
    third_sums = token_sums(2, third_out)
    split = split_z(keep, swap_dp(away), members, [partial_sent[0], output_piece])
    partial_sent = gate(partial_sent, split[1:2])
    scattered = scatter_z(split)
    summed = add_z(scattered, members, third_sums)
    summed = exchange(summed)
    piece = call(
        functools.partial(merge_body, members),
        (idx, *summed),
        "s" + "v" * members,
        [((slab, 3 * D), BF16)],
    )[0]
    output_pieces = gather_z(gate([output_piece], [piece])[0])
    out_parts += returns(2, third_sums)
    down_part = weight_grad(
        col_grad_body, grads_spot, grad_rows, blocks_gm, (inner, half_d), [piece]
    )
    away = [*gate([gate_part[1], up_part[1]], [piece]), down_part[1]]
    grad_gate, grad_up, grad_down = (
        (part[0] + swap_dp(peer).astype(F32))[None]
        for part, peer in zip((gate_part, up_part, down_part), away)
    )
    partial = exchange(partial_sent)
    last_out = exchange(gate(later_out[2], partial[1:]))
    last_sums = token_sums(3, last_out)
    block_out = residual + last_sums[0]
    for part in out_parts:
        block_out = block_out + part.astype(F32)
    block_out = block_out.astype(BF16)
    grad_in, line = call(
        functools.partial(input_body, members, experts),
        (idx, *partial, *small, hidden_in, grad_residual),
        "s" + "v" * (2 * members + 2),
        [((length, D), F32), ((8, D), F32)],
        scratch=[pltpu.VMEM((1, D), F32)],
        after=[piece],
    )

    small_part = jnp.concatenate([small_part[: experts + 1], line[:1]], axis=0)
    small_pieces = small_part.reshape(experts + 2, members, own).transpose(1, 0, 2)
    small_sum = at(small_pieces, me)
    for k in others:
        small_sum = small_sum + swap(at(small_pieces, me ^ k), k)
    small_sum = jnp.concatenate([small_sum, grad_gains[:2]], axis=0)
    small_sum = small_sum + swap_dp(small_sum)
    stack = jnp.stack(gather_z(small_sum))
    small_total = at(stack, (0 - mz) % planes)
    for z in range(1, planes):
        small_total = small_total + at(stack, (z - mz) % planes)
    output_sum = spread_z(output_pieces, 1)[0]
    grad_query, grad_key, grad_value_w = spread_z(gather_z(piece), 3)

    return (
        block_out,
        grad_in,
        small_total[experts + 1],
        small_total[experts + 2],
        small_total[experts + 3],
        small_total[experts],
        grad_query,
        grad_key,
        grad_value_w,
        output_sum,
        small_total[:experts].T,
        grad_gate,
        grad_up,
        grad_down,
    )


def solution(mesh):
    return jax.shard_map(
        shards,
        mesh=mesh,
        in_specs=(
            P(("dp", "expert", "shard"), None),
            P(("dp", "expert", "shard"), None),
            P(("dp", "expert"), None),
            P(("dp", "expert", "shard"), None),
            P("shard"),
            P("shard"),
            P("shard"),
            P("shard"),
            P("shard", None),
            P("shard", None),
            P("shard", None),
            P("shard", None),
            P("shard", None),
            P(("expert", "shard"), "dp", None),
            P(("expert", "shard"), "dp", None),
            P(("expert", "shard"), None, "dp"),
        ),
        out_specs=(
            P(("dp", "expert", "shard"), None),
            P(("dp", "expert", "shard"), None),
            P("shard"),
            P("shard"),
            P("shard"),
            P("shard"),
            P("shard", None),
            P("shard", None),
            P("shard", None),
            P("shard", None),
            P("shard", None),
            P(("expert", "shard"), "dp", None),
            P(("expert", "shard"), "dp", None),
            P(("expert", "shard"), None, "dp"),
        ),
        check_vma=False,
    )
```
